256 devices in a mesh: dp: 4 (over y_hi, core), corpus: 64 (over y_lo, x, z).
Axes of the slice: x: 4, y: 4 (y_hi: 2, y_lo: 2; y = y_hi * 2 + y_lo), z: 8, core: 2. Of those that a mesh axis runs over, the one named last changes fastest.
Arguments:
- queries: float32 [32768, 256], P(('dp', 'corpus')), may hold values from -40 to 40
- items: float32 [32768, 256], P('corpus'), may hold values from -6 to 6
- labels: int32 [32768], P(('dp', 'corpus')), may hold values from 0 to 32767
Outputs:
- loss: float32 [], replicated
- query_grad: float32 [32768, 256], P(('dp', 'corpus'))
- item_grad: float32 [32768, 256], P('corpus')
The draws below stay inside these ranges and needn't reach their ends.
All inputs are finite; a program needn't handle non-finite values.
Results may differ from the reference program's by a relative error of at most 0.0003.
Values sent between devices are 32-bit elements; how exact they have to be, the bound alone decides.
No kernel may reach another device: no remote copies, remote signals or barrier semaphores. Data moves between devices by JAX's collectives and lax.ppermute only.
A program may use at most 128 MiB of HBM per device.

```python
import math
import jax
import jax.numpy as jnp
from jax import lax

E = 256
NQ = 32768
NI = 32768


def paired_signs(key):
    signs = jax.random.rademacher(jax.random.fold_in(key, 50), (NI, E), dtype=jnp.float32)
    return jnp.repeat(signs.reshape(NI // 2, 2, E)[:, 0, :], 2, axis=0)


def place_items(base, plain):
    rows = jnp.arange(NI, dtype=jnp.int32)
    factor = jnp.where(rows % 2 == 1, 1.0 + 1.0 / 80.0, 1.0)
    aligned = rows % 64 < 2
    return jnp.where(aligned[:, None], base * factor[:, None], plain)


def heavy_rows(key, lowest):
    signs = jax.random.rademacher(jax.random.fold_in(key, 60), (NQ, E), dtype=jnp.float32)
    sizes = jax.random.uniform(jax.random.fold_in(key, 61), (NQ, E), jnp.float32, lowest, 40.0)
    return signs * sizes


def place_queries(base, plain, heavy):
    rows = jnp.arange(NQ, dtype=jnp.int32)
    group = rows // 64
    target = group * 7 % (NI // 64) * 64
    levels = jnp.array([110.0, 160.0, 215.0], jnp.float32)
    strength = levels[group % 3] * E ** (-0.5)
    matched = base[target] * strength[:, None]
    mixed = jnp.where((rows % 64 == 32)[:, None], heavy, plain)
    return jnp.where((rows % 64 == 0)[:, None], matched, mixed)


def draw_items(key, part):
    base = paired_signs(key)
    key = jax.random.fold_in(key, 1)
    plain = jax.random.truncated_normal(key, -6.0, 6.0, (NI, E), jnp.float32)
    return place_items(base, plain)


def draw_queries(key, part):
    base = paired_signs(key)
    key = jax.random.fold_in(key, 2)
    plain = jax.random.truncated_normal(key, -6.0, 6.0, (NQ, E), jnp.float32)
    heavy = heavy_rows(jax.random.fold_in(key, 3), 30.0)
    return place_queries(base, plain, heavy)


def with_ends(values, stream_key, least, high):
    longest = values.shape.index(max(values.shape))
    spots = []
    for shift in (0, 1):
        where = [jax.random.randint(jax.random.fold_in(stream_key, axis), (), 0, length) for axis, length in enumerate(values.shape)]
        where[longest] = (where[longest] + shift) % values.shape[longest]
        spots.append(tuple(where))
    return values.at[spots[0]].set(least).at[spots[1]].set(high)


def setup_inputs(seed: int = 0) -> dict:
    keys = jax.random.split(jax.random.key(seed), 4)
    queries = draw_queries(jax.random.fold_in(keys[3], 71), 0)
    items = draw_items(jax.random.fold_in(keys[3], 71), 0)
    labels = with_ends(jax.random.randint(keys[2], (NQ,), 0, NI), jax.random.fold_in(keys[2], 1), 0, NI - 1).astype(jnp.int32)
    return {"queries": queries, "items": items, "labels": labels}


def reference(queries, items, labels):
    scale = E ** -0.5
    block = math.gcd(NQ, 1024)
    count = NQ // block
    query_blocks = queries.reshape(count, block, E)
    label_blocks = labels.reshape(count, block)
    columns = jnp.arange(NI, dtype=jnp.int32)

    def score_block(query_rows):
        return jnp.dot(query_rows, items.T, precision=lax.Precision.HIGHEST) * scale

    def forward(pair):
        query_rows, label_rows = pair
        scores = score_block(query_rows)
        top = jnp.max(scores, axis=1)
        total = jnp.sum(jnp.exp(scores - top[:, None]), axis=1)
        picked = jnp.sum(jnp.where(columns[None, :] == label_rows[:, None], scores, 0.0), axis=1)
        return top + jnp.log(total), picked

    lse, picked = lax.map(forward, (query_blocks, label_blocks))
    loss = jnp.sum(lse - picked) / NQ

    def backward(accum, triple):
        query_rows, label_rows, lse_rows = triple
        scores = score_block(query_rows)
        delta = jnp.exp(scores - lse_rows[:, None]) - (columns[None, :] == label_rows[:, None]).astype(scores.dtype)
        grad_rows = jnp.dot(delta, items, precision=lax.Precision.HIGHEST) * scale
        accum = accum + jnp.dot(delta.T, query_rows, precision=lax.Precision.HIGHEST) * scale
        return accum, grad_rows

    start = jnp.zeros((NI, E), jnp.float32)
    item_grad, grad_blocks = lax.scan(backward, start, (query_blocks, label_blocks, lse))
    return loss, grad_blocks.reshape(NQ, E), item_grad
```

```python
import functools

import jax
import jax.numpy as jnp
from jax import lax
from jax.experimental import pallas as pl
from jax.experimental.pallas import tpu as pltpu
from jax.sharding import PartitionSpec as P

E = 256
ZN, XN, YN = 8, 4, 4
ROWS = 128
PAD = 136
HALF = 256
PIECES = 8
LOCAL = PIECES * HALF
AXES = ("dp", "corpus")
f32, bf16 = jnp.float32, jnp.bfloat16


def place(i):
    return (i >> 7) & 1, (i >> 6) & 1, (i >> 5) & 1, (i >> 3) & 3, i & 7


def index(yh, c, yl, x, z):
    return yh * 128 + c * 64 + yl * 32 + x * 8 + z


def pairs(dx=0, dy=0, dz=0, dc=0):
    out = []
    for i in range(256):
        yh, c, yl, x, z = place(i)
        y = (yh * 2 + yl + dy) % YN
        out.append((i, index(y >> 1, (c + dc) % 2, y & 1, (x + dx) % XN, (z + dz) % ZN)))
    return out


def send(a, **shift):
    return lax.ppermute(a, AXES, pairs(**shift))


def flip(a, bit):
    return lax.ppermute(a, AXES, [(i, i ^ bit) for i in range(256)])


def split(a):
    hi = a.astype(bf16)
    return hi, (a - hi.astype(f32)).astype(bf16)


def dot(a, b, dims):
    return lax.dot_general(a, b, (dims, ((), ())), preferred_element_type=f32)


NT = ((1,), (1,))
NN = ((1,), (0,))


def local_labels(pos_ref, mine_ref, other_ref):
    lab = jnp.concatenate(
        [mine_ref[0, ROWS : ROWS + 1, :ROWS], other_ref[0, ROWS : ROWS + 1, :ROWS]], axis=1
    ).astype(jnp.int32)
    z, c, yl, x = pos_ref[0], pos_ref[1], pos_ref[2], pos_ref[3]
    here = ((lab >> 9) & 7 == z) & ((lab >> 8) & 1 == c)
    piece = (((lab >> 14) ^ yl) & 1) * 4 + (((lab >> 12) & 3) - x & 3)
    return jnp.where(here, piece * HALF + (lab & 255), -1)


def query_rows(mine_ref, other_ref):
    return jnp.concatenate([mine_ref[0, :ROWS, :], other_ref[0, :ROWS, :]], axis=0) * (E**-0.5)


def forward_kernel(pos_ref, x_ref, mine_ref, other_ref, s_ref, stat_ref, xh, xl):
    @pl.when(pl.program_id(0) == 0)
    def _():
        xh[...], xl[...] = split(x_ref[...])

    qh, ql = split(query_rows(mine_ref, other_ref))
    lab = local_labels(pos_ref, mine_ref, other_ref)
    rows = lax.broadcasted_iota(jnp.int32, (HALF, 256), 0)
    top = total = None
    pick = jnp.zeros((8, 256), f32)
    for t in range(PIECES):
        at = slice(t * HALF, (t + 1) * HALF)
        s = dot(xh[at], qh, NT) + (dot(xl[at], qh, NT) + dot(xh[at], ql, NT))
        s_ref[0, at, :] = s
        pick += jnp.sum(jnp.where(rows == lab - t * HALF, s, 0.0).reshape(32, 8, 256), axis=0)
        s = s.reshape(32, 8, 256)
        best = jnp.max(s, axis=0)
        if top is None:
            total = jnp.sum(jnp.exp(s - best[None]), axis=0)
            top = best
        else:
            best = jnp.maximum(top, best)
            total = total * jnp.exp(top - best) + jnp.sum(jnp.exp(s - best[None]), axis=0)
            top = best
    best = jnp.max(top, axis=0, keepdims=True)
    stat_ref[0, 0:1, :] = best
    stat_ref[0, 1:2, :] = jnp.sum(total * jnp.exp(top - best), axis=0, keepdims=True)
    stat_ref[0, 2:3, :] = jnp.sum(pick, axis=0, keepdims=True)


def backward_kernel(pos_ref, x_ref, mine_ref, other_ref, lse_ref, s_ref, o_ref, g_ref, xth, xtl, g_acc):
    step = pl.program_id(0)

    @pl.when(step == 0)
    def _():
        for t in range(PIECES):
            at = slice(t * HALF, (t + 1) * HALF)
            xth[:, at], xtl[:, at] = split(x_ref[at, :].T)
        g_acc[...] = jnp.zeros_like(g_acc)

    qh, ql = split(query_rows(mine_ref, other_ref))
    lab = local_labels(pos_ref, mine_ref, other_ref)
    lse = lse_ref[0]
    rows = lax.broadcasted_iota(jnp.int32, (HALF, 256), 0)
    ot = jnp.zeros((E, 256), f32)
    for t in range(PIECES):
        at = slice(t * HALF, (t + 1) * HALF)
        p = jnp.exp(s_ref[0, at, :] - lse)
        dh, dl = split(jnp.where(rows == lab - t * HALF, p - 1.0, p))
        g_acc[at, :] += dot(dh, qh, NN) + (dot(dh, ql, NN) + dot(dl, qh, NN))
        ot += dot(xth[:, at], dh, NN) + (dot(xtl[:, at], dh, NN) + dot(xth[:, at], dl, NN))
    o_ref[0] = ot.T * (E**-0.5)

    @pl.when(step == ZN - 1)
    def _():
        g_ref[...] = g_acc[...]


def params(mib):
    return pltpu.CompilerParams(vmem_limit_bytes=mib * 2**20, dimension_semantics=("arbitrary",))


def slot(i, pos):
    return lax.rem(i - pos[0] + ZN, ZN)


X_SPEC = pl.BlockSpec((LOCAL, E), lambda i, pos: (0, 0))
Q_SPEC = pl.BlockSpec((1, PAD, E), lambda i, pos: (slot(i, pos), 0, 0))
S_SPEC = pl.BlockSpec((1, LOCAL, 256), lambda i, pos: (i, 0, 0))


def forward(pos, x, mine, other):
    return pl.pallas_call(
        forward_kernel,
        grid_spec=pltpu.PrefetchScalarGridSpec(
            num_scalar_prefetch=1,
            grid=(ZN,),
            in_specs=[X_SPEC, Q_SPEC, Q_SPEC],
            out_specs=[S_SPEC, pl.BlockSpec((1, 3, 256), lambda i, pos: (i, 0, 0))],
            scratch_shapes=[pltpu.VMEM((LOCAL, E), bf16), pltpu.VMEM((LOCAL, E), bf16)],
        ),
        out_shape=[
            jax.ShapeDtypeStruct((ZN, LOCAL, 256), f32),
            jax.ShapeDtypeStruct((ZN, 3, 256), f32),
        ],
        compiler_params=params(40),
        cost_estimate=pl.CostEstimate(flops=3 * 2**31, bytes_accessed=22 * 2**20, transcendentals=2**22),
        name="forward",
    )(pos, x, mine, other)


def backward(pos, x, mine, other, lse, s):
    return pl.pallas_call(
        backward_kernel,
        grid_spec=pltpu.PrefetchScalarGridSpec(
            num_scalar_prefetch=1,
            grid=(ZN,),
            in_specs=[X_SPEC, Q_SPEC, Q_SPEC, pl.BlockSpec((1, 1, 256), lambda i, pos: (i, 0, 0)), S_SPEC],
            out_specs=[
                pl.BlockSpec((1, 256, E), lambda i, pos: (slot(i, pos), 0, 0)),
                pl.BlockSpec((LOCAL, E), lambda i, pos: (0, 0)),
            ],
            scratch_shapes=[
                pltpu.VMEM((E, LOCAL), bf16),
                pltpu.VMEM((E, LOCAL), bf16),
                pltpu.VMEM((LOCAL, E), f32),
            ],
        ),
        out_shape=[
            jax.ShapeDtypeStruct((ZN, 256, E), f32),
            jax.ShapeDtypeStruct((LOCAL, E), f32),
        ],
        compiler_params=params(48),
        cost_estimate=pl.CostEstimate(flops=6 * 2**31, bytes_accessed=26 * 2**20, transcendentals=2**22),
        name="backward",
    )(pos, x, mine, other, lse, s)


def gather_queries(q):
    cut = 64
    r1, l1 = send(q, dz=1), send(q, dz=-1)
    r2, l2 = send(r1, dz=1), send(l1, dz=-1)
    r3, l3 = send(r2, dz=1), send(l2, dz=-1)
    r4, l4 = send(r3[:cut], dz=1), send(l3[cut:], dz=-1)
    return jnp.concatenate([q, l1, l2, l3, r4, l4, r3, r2, r1], axis=0).reshape(ZN, PAD, E)


def gather_items(own):
    cut = HALF // 2
    ya, yb = send(own[:cut], dy=-1), send(own[cut:], dy=1)
    r1, l1 = send(own, dx=1), send(own, dx=-1)
    r2, l2 = send(r1[:cut], dx=1), send(l1[cut:], dx=-1)
    yl1, yr1 = send(l1, dy=-1), send(r1, dy=1)
    yr2, yl2 = send(r2, dy=-1), send(l2, dy=1)
    return jnp.concatenate([own, l1, r2, l2, r1, ya, yb, yl1, yr2, yl2, yr1], axis=0)


def merge(a, b):
    first = a[:, 0] >= b[:, 0]
    best, least = jnp.where(first, a[:, 0], b[:, 0]), jnp.where(first, b[:, 0], a[:, 0])
    total, rest = jnp.where(first, a[:, 1], b[:, 1]), jnp.where(first, b[:, 1], a[:, 1])
    return jnp.stack([best, total + rest * jnp.exp(least - best), a[:, 2] + b[:, 2]], axis=1)


def exchange_stats(stat):
    got = send(stat, dc=1)
    stat = merge(stat, jnp.concatenate([got[:, :, ROWS:], got[:, :, :ROWS]], axis=2))
    for bit in (1, 2, 4):
        stat = merge(stat, flip(stat, bit))
    return stat


def scatter_queries(o):
    cut = 64
    o = o[:, :ROWS] + send(o[:, ROWS:], dc=1)
    up, down = send(o[4, :cut], dz=1), send(o[4, cut:], dz=-1)
    up = jnp.concatenate([o[3, :cut] + up, o[3, cut:]], axis=0)
    down = jnp.concatenate([o[5, :cut], o[5, cut:] + down], axis=0)
    up, down = send(up, dz=1), send(down, dz=-1)
    up, down = send(o[2] + up, dz=1), send(o[6] + down, dz=-1)
    up, down = send(o[1] + up, dz=1), send(o[7] + down, dz=-1)
    return o[0] + up + down


def scatter_items(g, core):
    cut = HALF // 2
    g = g.reshape(2, 4, HALF, E)
    a, b = send(g[1, :, :cut], dy=1), send(g[1, :, cut:], dy=-1)
    up, down = send(g[0, 2, :cut] + a[2], dx=1), send(g[0, 2, cut:] + b[2], dx=-1)
    got = jnp.concatenate([a, b], axis=1)
    up = g[0, 1] + got[1] + jnp.pad(up, ((0, cut), (0, 0)))
    down = g[0, 3] + got[3] + jnp.pad(down, ((cut, 0), (0, 0)))
    up, down = send(up, dx=1), send(down, dx=-1)
    mine = g[0, 0] + got[0] + up + down
    mine = mine + send(mine, dy=2)
    other = send(mine, dc=1)
    return jnp.where(core == 0, jnp.concatenate([mine, other]), jnp.concatenate([other, mine]))


def body(queries, items, labels):
    _, core, y_lo, x_at, z_at = place(lax.axis_index("dp") * 64 + lax.axis_index("corpus"))
    pos = jnp.stack([z_at, core, y_lo, x_at]).astype(jnp.int32)
    row = jnp.pad(labels.astype(f32).reshape(1, ROWS), ((0, PAD - ROWS - 1), (0, E - ROWS)))
    mine = gather_queries(jnp.concatenate([queries, row], axis=0))
    other = send(mine, dc=1)
    x = gather_items(lax.dynamic_slice_in_dim(items, core * HALF, HALF))
    s, stat = forward(pos, x, mine, other)
    stat = exchange_stats(stat)
    lse = stat[:, 0] + jnp.log(stat[:, 1])
    part = jnp.sum(lse - stat[:, 2], axis=0)
    part = jnp.sum(part[:ROWS] + part[ROWS:])
    o, g = backward(pos, x, mine, other, lse[:, None], s)
    query_grad = scatter_queries(o)
    item_grad = scatter_items(g, core)
    for bit in (8, 16, 32, 128):
        part = part + flip(part, bit)
    return part / 32768, query_grad, item_grad


def solution(mesh):
    in_specs = (P(AXES, None), P("corpus", None), P(AXES))
    out_specs = (P(), P(AXES, None), P("corpus", None))
    return jax.shard_map(body, mesh=mesh, in_specs=in_specs, out_specs=out_specs, check_vma=False)
```

```python
import jax
import jax.numpy as jnp
from jax import lax
from jax.experimental import pallas as pl
from jax.experimental.pallas import tpu as pltpu
from jax.sharding import Mesh, PartitionSpec as P

E = 256
ZN, XN, YN = 8, 4, 4
ROWS = 128
PAD = 136
HALF = 256
CUT = HALF // 2
PIECES = 8
LOCAL = PIECES * HALF
AXES = ("yh", "c", "yl", "x", "z")
f32, bf16 = jnp.float32, jnp.bfloat16


def place(i):
    return (i >> 7) & 1, (i >> 6) & 1, (i >> 5) & 1, (i >> 3) & 3, i & 7


def index(yh, c, yl, x, z):
    return yh * 128 + c * 64 + yl * 32 + x * 8 + z


def pairs(dx=0, dy=0, dz=0, dc=0):
    out = []
    for i in range(256):
        yh, c, yl, x, z = place(i)
        y = (yh * 2 + yl + dy) % YN
        out.append((i, index(y >> 1, (c + dc) % 2, y & 1, (x + dx) % XN, (z + dz) % ZN)))
    return out


def send(a, **shift):
    return lax.ppermute(a, AXES, pairs(**shift))


def flip(a, bit):
    return lax.ppermute(a, AXES, [(i, i ^ bit) for i in range(256)])


def after(a, b):
    return lax.optimization_barrier((a, b))[0]


def split(a):
    hi = a.astype(bf16)
    return hi, (a - hi.astype(f32)).astype(bf16)


def dot(a, b, dims):
    return lax.dot_general(a, b, (dims, ((), ())), preferred_element_type=f32)


def cat(parts, axis):
    return jnp.concatenate(parts, axis=axis)


NT = ((1,), (1,))
NN = ((1,), (0,))
SMEM = pl.BlockSpec(memory_space=pltpu.SMEM)
VMEM = pl.BlockSpec(memory_space=pltpu.VMEM)


def shape(*dims, dtype=f32):
    return jax.ShapeDtypeStruct(dims, dtype)


def params(mib):
    return pltpu.CompilerParams(vmem_limit_bytes=mib * 2**20)


def local_labels(pos_ref, q_ref):
    lab = cat([q_ref[0, ROWS : ROWS + 1, :ROWS], q_ref[1, ROWS : ROWS + 1, :ROWS]], 1)
    lab = lab.astype(jnp.int32)
    z, c, yl, x = pos_ref[0], pos_ref[1], pos_ref[2], pos_ref[3]
    here = ((lab >> 9) & 7 == z) & ((lab >> 8) & 1 == c)
    piece = (((lab >> 14) ^ yl) & 1) * 4 + (((lab >> 12) & 3) - x & 3)
    return jnp.where(here, piece * HALF + (lab & 255), -1)


def query_rows(q_ref):
    return cat([q_ref[0, :ROWS, :], q_ref[1, :ROWS, :]], 0) * (E**-0.5)


def small(kernel, ins, outs, smem_out=()):
    return pl.pallas_call(
        kernel,
        in_specs=[SMEM if a.ndim == 1 else VMEM for a in ins],
        out_specs=[SMEM if len(o.shape) == 1 else VMEM for o in outs],
        out_shape=outs,
        compiler_params=params(10),
        name=kernel.__name__,
    )(*ins)


def start_kernel(pos_ref, queries, labels, items, out, own):
    for k in range(ZN):
        out[k, :ROWS, :] = queries[...]
        out[k, ROWS:, :ROWS] = jnp.broadcast_to(labels[...].astype(f32), (PAD - ROWS, ROWS))
        out[k, ROWS:, ROWS:] = jnp.zeros((PAD - ROWS, E - ROWS), f32)
    own[...] = items[pl.ds(pl.multiple_of(pos_ref[1] * HALF, HALF), HALF), :]


def pack_items_kernel(*refs):
    *parts, xh, xl, xth, xtl, token = refs
    token[0] = 0.0
    for d, p in enumerate(parts):
        at = slice(d * HALF, (d + 1) * HALF)
        xh[at, :], xl[at, :] = split(p[...])
        xth[:, at], xtl[:, at] = split(p[...].T)


def hold_kernel(token, a, out):
    out[...] = a[...]


def spread_kernel(mine, other, out):
    for k in range(2 * ZN):
        out[k, 0] = mine[...]
        out[k, 1] = other[...]


def merge_kernel(pos_ref, got, lse_ref, part_ref):
    core = pos_ref[1]
    loss = None
    for h in range(2):
        side = [(k, h ^ ((core ^ (k // ZN)) & 1)) for k in range(2 * ZN)]
        best = got[side[0][0], side[0][1], 0]
        for k, w in side[1:]:
            best = jnp.maximum(best, got[k, w, 0])
        total = pick = jnp.zeros((ZN, ROWS), f32)
        for k, w in side:
            total += got[k, w, 1] * jnp.exp(got[k, w, 0] - best)
            pick += got[k, w, 2]
        lse = best + jnp.log(total)
        lse_ref[h] = lse
        loss = lse - pick if loss is None else loss + (lse - pick)
    part_ref[0] = jnp.sum(loss)


def forward_kernel(pos_ref, xh, xl, q_ref, s0_ref, s1_ref, stat_ref):
    qh, ql = split(query_rows(q_ref))
    qcat = cat([qh, qh, ql], 1)
    lab = local_labels(pos_ref, q_ref)
    rows = lax.broadcasted_iota(jnp.int32, (HALF, 256), 0)
    top = total = None
    pick = jnp.zeros((8, 256), f32)
    for t in range(PIECES):
        at = slice(t * HALF, (t + 1) * HALF)
        s = dot(cat([xh[at], xl[at], xh[at]], 1), qcat, NT)
        (s0_ref, s1_ref)[t // 4][0, t % 4] = s
        pick += jnp.sum(jnp.where(rows == lab - t * HALF, s, 0.0).reshape(32, 8, 256), axis=0)
        s = s.reshape(32, 8, 256)
        best = jnp.max(s, axis=0)
        if top is None:
            total = jnp.sum(jnp.exp(s - best[None]), axis=0)
        else:
            best = jnp.maximum(top, best)
            total = total * jnp.exp(top - best) + jnp.sum(jnp.exp(s - best[None]), axis=0)
        top = best
    best = jnp.max(top, axis=0, keepdims=True)
    total = jnp.sum(total * jnp.exp(top - best), axis=0, keepdims=True)
    pick = jnp.sum(pick, axis=0, keepdims=True)
    for h in range(2):
        z = 2 * pl.program_id(0) + h
        at = slice(h * ROWS, (h + 1) * ROWS)
        stat_ref[0, pl.ds(z, 1), :] = best[:, at]
        stat_ref[1, pl.ds(z, 1), :] = total[:, at]
        stat_ref[2, pl.ds(z, 1), :] = pick[:, at]


def forward(pos, xh, xl, q):
    return pl.pallas_call(
        forward_kernel,
        grid=(4,),
        in_specs=[
            SMEM,
            pl.BlockSpec((LOCAL, E), lambda i: (0, 0)),
            pl.BlockSpec((LOCAL, E), lambda i: (0, 0)),
            pl.BlockSpec((2, PAD, E), lambda i: (i, 0, 0)),
        ],
        out_specs=[
            pl.BlockSpec((1, 4, HALF, 256), lambda i: (i, 0, 0, 0)),
            pl.BlockSpec((1, 4, HALF, 256), lambda i: (i, 0, 0, 0)),
            pl.BlockSpec((3, ZN, ROWS), lambda i: (0, 0, 0)),
        ],
        out_shape=[shape(4, 4, HALF, 256)] * 2 + [shape(3, ZN, ROWS)],
        compiler_params=params(12),
        cost_estimate=pl.CostEstimate(flops=3 * 2**30, bytes_accessed=10 * 2**20, transcendentals=2**21),
        name="forward",
    )(pos, xh, xl, q)


def delta(s, lse, rows, lab, at):
    p = jnp.exp(s - lse)
    return split(jnp.where(rows == lab - at, p - 1.0, p))


def block(i, pos_ref, lse_ref, mine, other):
    q = jnp.where(i < 4, mine[...], other[...])
    qh, ql = split(query_rows(q))
    z = 2 * (i & 3)
    k = i >> 2
    lse = cat([lse_ref[k, pl.ds(z, 1), :], lse_ref[k, pl.ds(z + 1, 1), :]], 1)
    return cat([qh, ql, qh], 0), local_labels(pos_ref, q), lse


def backward_a_kernel(pos_ref, part, xth, xtl, mine, other, lse_ref, sm0, sm1, so0, so1, om, oo, up, down, token, g_acc):
    i = pl.program_id(0)

    @pl.when(i == 0)
    def _():
        g_acc[...] = jnp.zeros_like(g_acc)
        token[0] = 0.0

    qcat, lab, lse = block(i, pos_ref, lse_ref, mine, other)
    rows = lax.broadcasted_iota(jnp.int32, (HALF, 256), 0)
    ot = jnp.zeros((E, 256), f32)
    for t in range(PIECES):
        at = slice(t * HALF, (t + 1) * HALF)
        sm, so = ((sm0, so0), (sm1, so1))[t // 4]
        dh, dl = delta(jnp.where(i < 4, sm[0, t % 4], so[0, t % 4]), lse, rows, lab, t * HALF)
        if t >= 4:
            g_acc[t - 4] += dot(cat([dh, dh, dl], 1), qcat, NN)
        ot += dot(cat([xth[:, at], xtl[:, at], xth[:, at]], 1), cat([dh, dh, dl], 0), NN)
    o = ot.T * (E**-0.5)

    @pl.when(i < 4)
    def _():
        om[2 * i], om[2 * i + 1] = o[:ROWS], o[ROWS:]

    @pl.when(i >= 4)
    def _():
        oo[2 * i - ZN], oo[2 * i - ZN + 1] = o[:ROWS], o[ROWS:]

    @pl.when(i == ZN - 1)
    def _():
        for d in range(4):
            up[d * CUT : (d + 1) * CUT, :] = g_acc[d, :CUT, :]
            down[d * CUT : (d + 1) * CUT, :] = g_acc[d, CUT:, :]
        up[4 * CUT :, :] = down[4 * CUT :, :] = jnp.full((8, E), part[0], f32)


def backward_b_kernel(pos_ref, token, mine, other, lse_ref, sm0, so0, g_ref):
    i = pl.program_id(0)

    @pl.when(i == 0)
    def _():
        g_ref[...] = jnp.zeros_like(g_ref)

    qcat, lab, lse = block(i, pos_ref, lse_ref, mine, other)
    rows = lax.broadcasted_iota(jnp.int32, (HALF, 256), 0)
    for t in range(4):
        dh, dl = delta(jnp.where(i < 4, sm0[0, t], so0[0, t]), lse, rows, lab, t * HALF)
        g_ref[t] += dot(cat([dh, dh, dl], 1), qcat, NN)


Q_SPECS = [
    pl.BlockSpec((2, PAD, E), lambda i: (jnp.minimum(i, 3), 0, 0)),
    pl.BlockSpec((2, PAD, E), lambda i: (jnp.maximum(i, 4) - 4, 0, 0)),
    pl.BlockSpec((2, ZN, ROWS), lambda i: (0, 0, 0)),
]


SM_SPEC = pl.BlockSpec((1, 4, HALF, 256), lambda i: (jnp.minimum(i, 3), 0, 0, 0))
SO_SPEC = pl.BlockSpec((1, 4, HALF, 256), lambda i: (jnp.maximum(i, 4) - 4, 0, 0, 0))


def backward_a(pos, part, xth, xtl, mine, other, lse, *s):
    whole = lambda *dims: pl.BlockSpec(dims, lambda i: (0,) * len(dims))
    return pl.pallas_call(
        backward_a_kernel,
        grid=(ZN,),
        in_specs=[SMEM, SMEM, whole(E, LOCAL), whole(E, LOCAL), *Q_SPECS]
        + [SM_SPEC, SM_SPEC, SO_SPEC, SO_SPEC],
        out_specs=[whole(ZN, ROWS, E)] * 2 + [whole(4 * CUT + 8, E)] * 2 + [SMEM],
        out_shape=[shape(ZN, ROWS, E)] * 2 + [shape(4 * CUT + 8, E)] * 2 + [shape(1)],
        scratch_shapes=[pltpu.VMEM((4, HALF, E), f32)],
        compiler_params=params(14),
        cost_estimate=pl.CostEstimate(flops=9 * 2**30, bytes_accessed=22 * 2**20, transcendentals=2**22),
        name="backward_a",
    )(pos, part, xth, xtl, mine, other, lse, *s)


def backward_b(pos, token, mine, other, lse, *s):
    return pl.pallas_call(
        backward_b_kernel,
        grid=(ZN,),
        in_specs=[SMEM, SMEM, *Q_SPECS, SM_SPEC, SO_SPEC],
        out_specs=pl.BlockSpec((4, HALF, E), lambda i: (0, 0, 0)),
        out_shape=shape(4, HALF, E),
        compiler_params=params(14),
        cost_estimate=pl.CostEstimate(flops=3 * 2**30, bytes_accessed=11 * 2**20, transcendentals=2**21),
        name="backward_b",
    )(pos, token, mine, other, lse, *s)


def gather(qs, own):
    mine = lax.all_to_all(qs, "z", 0, 0, tiled=True)
    y0, x3, x1 = flip(own, 32), send(own, dx=1), send(own, dx=-1)
    y0, x3, x1 = lax.optimization_barrier((y0, x3, x1))
    y3, y1, x2 = send(y0, dx=1), send(y0, dx=-1), send(x3, dx=1)
    y3, y1, x2 = lax.optimization_barrier((y3, y1, x2))
    y2 = send(y1, dx=-1)
    return mine, [own, x1, x2, x3, y0, y1, y2, y3]


def fold_kernel(part, g, a, b, *out):
    for d in range(4):
        at = slice(d * CUT, (d + 1) * CUT)
        out[d][:CUT] = g[d, :CUT] + a[at]
        out[d][CUT:HALF] = g[d, CUT:] + b[at]
        out[d][HALF : HALF + 1] = jnp.full((1, E), part[0], f32)
        out[d][HALF + 1 : HALF + 2] = a[4 * CUT : 4 * CUT + 1]
        out[d][HALF + 2 : HALF + 3] = b[4 * CUT : 4 * CUT + 1]
        out[d][HALF + 3 :] = jnp.zeros((5, E), f32)


def land_kernel(m0, m1, m2, m3, out):
    out[...] = (m0[...] + m2[...]) + (m1[...] + m3[...])


def join_kernel(pos_ref, mine, mine2, other, other2, out, loss):
    c = pos_ref[1]
    out[pl.ds(pl.multiple_of(c * HALF, HALF), HALF), :] = mine[:HALF] + mine2[:HALF]
    out[pl.ds(pl.multiple_of((1 - c) * HALF, HALF), HALF), :] = other[:HALF] + other2[:HALF]
    total = (mine[HALF : HALF + 1] + mine2[HALF : HALF + 1]) + (
        mine[HALF + 1 : HALF + 2] + mine[HALF + 2 : HALF + 3]
    )
    loss[0] = jnp.max(total) / 32768


def sum_kernel(got, out):
    total = got[0]
    for k in range(1, ZN):
        total += got[k]
    out[...] = total


def add_kernel(a, b, out):
    out[...] = a[...] + b[...]


def body(queries, items, labels):
    core, y_lo, x_at, z_at = (lax.axis_index(a) for a in ("c", "yl", "x", "z"))
    pos = jnp.stack([z_at, core, y_lo, x_at]).astype(jnp.int32)
    qs, own = small(
        start_kernel, [pos, queries, labels.reshape(1, ROWS), items], [shape(ZN, PAD, E), shape(HALF, E)]
    )
    mine, parts = gather(qs, own)
    xh, xl, xth, xtl, packed = small(
        pack_items_kernel,
        parts,
        [shape(LOCAL, E, dtype=bf16)] * 2 + [shape(E, LOCAL, dtype=bf16)] * 2 + [shape(1)],
    )
    (mine,) = small(hold_kernel, [packed, mine], [shape(ZN, PAD, E)])
    other = send(mine, dc=1)
    sm0, sm1, stat_m = forward(pos, xh, xl, mine)
    so0, so1, stat_o = forward(pos, xh, xl, other)
    (stats,) = small(spread_kernel, [stat_m, stat_o], [shape(2 * ZN, 2, 3, ZN, ROWS)])
    stats = lax.all_to_all(stats, ("c", "z"), 0, 0, tiled=True)
    lse, part = small(merge_kernel, [pos, stats], [shape(2, ZN, ROWS), shape(1)])
    om, oo, up, down, first = backward_a(pos, part, xth, xtl, mine, other, lse, sm0, sm1, so0, so1)
    a, b = send(up, dy=1), send(down, dy=-1)
    g = backward_b(pos, first, mine, other, lse, sm0, so0)
    (o,) = small(add_kernel, [om, send(oo, dc=1)], [shape(ZN, ROWS, E)])
    o = lax.all_to_all(o, "z", 0, 0, tiled=True)
    m0, m1, m2, m3 = small(fold_kernel, [part, g, a, b], [shape(HALF + 8, E)] * 4)
    m2, m1, m3 = send(m2, dx=2), send(m1, dx=1), send(m3, dx=-1)
    (own,) = small(land_kernel, [m0, m1, m2, m3], [shape(HALF + 8, E)])
    got = send(own, dy=2)
    near = send(own, dc=1)
    item_grad, loss = small(
        join_kernel, [pos, own, got, near, send(got, dc=1)], [shape(2 * HALF, E), shape(1)]
    )
    (query_grad,) = small(sum_kernel, [o], [shape(ROWS, E)])
    return loss.reshape(()), query_grad, item_grad


def solution(mesh):
    grid = Mesh(mesh.devices.reshape(2, 2, 2, 4, 8), AXES)
    corpus = ("yl", "x", "z")
    in_specs = (P(AXES, None), P(corpus, None), P(AXES))
    out_specs = (P(), P(AXES, None), P(corpus, None))
    return jax.shard_map(body, mesh=grid, in_specs=in_specs, out_specs=out_specs, check_vma=False)
```

```python
import jax
import jax.numpy as jnp
from jax import lax
from jax.experimental import pallas as pl
from jax.experimental.pallas import tpu as pltpu
from jax.sharding import Mesh, PartitionSpec as P

E = 256
ZN, XN, YN = 8, 4, 4
ROWS = 128
PAD = 136
HALF = 256
CUT = HALF // 2
PIECES = 8
LOCAL = PIECES * HALF
AXES = ("yh", "c", "yl", "x", "z")
f32, bf16 = jnp.float32, jnp.bfloat16


def place(i):
    return (i >> 7) & 1, (i >> 6) & 1, (i >> 5) & 1, (i >> 3) & 3, i & 7


def index(yh, c, yl, x, z):
    return yh * 128 + c * 64 + yl * 32 + x * 8 + z


def pairs(dx=0, dy=0, dz=0, dc=0):
    out = []
    for i in range(256):
        yh, c, yl, x, z = place(i)
        y = (yh * 2 + yl + dy) % YN
        out.append((i, index(y >> 1, (c + dc) % 2, y & 1, (x + dx) % XN, (z + dz) % ZN)))
    return out


def send(a, **shift):
    return lax.ppermute(a, AXES, pairs(**shift))


def flip(a, bit):
    return lax.ppermute(a, AXES, [(i, i ^ bit) for i in range(256)])


def split(a):
    hi = a.astype(bf16)
    return hi, (a - hi.astype(f32)).astype(bf16)


def dot(a, b, dims):
    return lax.dot_general(a, b, (dims, ((), ())), preferred_element_type=f32)


def cat(parts, axis):
    return jnp.concatenate(parts, axis=axis)


NT = ((1,), (1,))
NN = ((1,), (0,))
TN = ((0,), (0,))
SMEM = pl.BlockSpec(memory_space=pltpu.SMEM)
VMEM = pl.BlockSpec(memory_space=pltpu.VMEM)


def shape(*dims, dtype=f32):
    return jax.ShapeDtypeStruct(dims, dtype)


def params(mib):
    return pltpu.CompilerParams(vmem_limit_bytes=mib * 2**20)


def local_labels(pos_ref, q_ref):
    lab = cat([q_ref[0, ROWS : ROWS + 1, :ROWS], q_ref[1, ROWS : ROWS + 1, :ROWS]], 1)
    lab = lab.astype(jnp.int32)
    z, c, yl, x = pos_ref[0], pos_ref[1], pos_ref[2], pos_ref[3]
    here = ((lab >> 9) & 7 == z) & ((lab >> 8) & 1 == c)
    piece = (((lab >> 14) ^ yl) & 1) * 4 + (((lab >> 12) & 3) - x & 3)
    return jnp.where(here, piece * HALF + (lab & 255), -1)


def query_rows(q_ref):
    return cat([q_ref[0, :ROWS, :], q_ref[1, :ROWS, :]], 0) * (E**-0.5)


def small(kernel, ins, outs, smem_out=()):
    return pl.pallas_call(
        kernel,
        in_specs=[SMEM if a.ndim == 1 else VMEM for a in ins],
        out_specs=[SMEM if len(o.shape) == 1 else VMEM for o in outs],
        out_shape=outs,
        compiler_params=params(10),
        name=kernel.__name__,
    )(*ins)


def start_kernel(pos_ref, queries, labels, items, out, own):
    for k in range(ZN):
        out[k, :ROWS, :] = queries[...]
        out[k, ROWS:, :ROWS] = jnp.broadcast_to(labels[...].astype(f32), (PAD - ROWS, ROWS))
        out[k, ROWS:, ROWS:] = jnp.zeros((PAD - ROWS, E - ROWS), f32)
    own[...] = items[pl.ds(pl.multiple_of(pos_ref[1] * HALF, HALF), HALF), :]


def pack_items_kernel(*refs):
    *parts, mine, xh, xl, held = refs
    held[...] = mine[...]
    for d, p in enumerate(parts):
        at = slice(d * HALF, (d + 1) * HALF)
        xh[at, :], xl[at, :] = split(p[...])


def spread_kernel(mine, other, out):
    for k in range(2 * ZN):
        out[k, 0] = mine[...]
        out[k, 1] = other[...]


def merge_kernel(pos_ref, got, lse_ref, part_ref):
    core = pos_ref[1]
    loss = None
    for h in range(2):
        side = [(k, h ^ ((core ^ (k // ZN)) & 1)) for k in range(2 * ZN)]
        best = got[side[0][0], side[0][1], 0]
        for k, w in side[1:]:
            best = jnp.maximum(best, got[k, w, 0])
        total = pick = jnp.zeros((ZN, ROWS), f32)
        for k, w in side:
            total += got[k, w, 1] * jnp.exp(got[k, w, 0] - best)
            pick += got[k, w, 2]
        lse = best + jnp.log(total)
        lse_ref[h] = lse
        loss = lse - pick if loss is None else loss + (lse - pick)
    part_ref[0] = jnp.sum(loss)


def forward_kernel(pos_ref, xh, xl, q_ref, s0_ref, s1_ref, stat_ref):
    qh, ql = split(query_rows(q_ref))
    qcat = cat([qh, qh, ql], 1)
    lab = local_labels(pos_ref, q_ref)
    rows = lax.broadcasted_iota(jnp.int32, (HALF, 256), 0)
    top = total = None
    pick = jnp.zeros((8, 256), f32)
    for t in range(PIECES):
        at = slice(t * HALF, (t + 1) * HALF)
        s = dot(cat([xh[at], xl[at], xh[at]], 1), qcat, NT)
        (s0_ref, s1_ref)[t // 4][0, t % 4] = s
        pick += jnp.sum(jnp.where(rows == lab - t * HALF, s, 0.0).reshape(32, 8, 256), axis=0)
        s = s.reshape(32, 8, 256)
        best = jnp.max(s, axis=0)
        if top is None:
            total = jnp.sum(jnp.exp(s - best[None]), axis=0)
        else:
            best = jnp.maximum(top, best)
            total = total * jnp.exp(top - best) + jnp.sum(jnp.exp(s - best[None]), axis=0)
        top = best
    best = jnp.max(top, axis=0, keepdims=True)
    total = jnp.sum(total * jnp.exp(top - best), axis=0, keepdims=True)
    pick = jnp.sum(pick, axis=0, keepdims=True)
    for h in range(2):
        z = 2 * pl.program_id(0) + h
        at = slice(h * ROWS, (h + 1) * ROWS)
        stat_ref[0, pl.ds(z, 1), :] = best[:, at]
        stat_ref[1, pl.ds(z, 1), :] = total[:, at]
        stat_ref[2, pl.ds(z, 1), :] = pick[:, at]


def forward(pos, xh, xl, q):
    return pl.pallas_call(
        forward_kernel,
        grid=(4,),
        in_specs=[
            SMEM,
            pl.BlockSpec((LOCAL, E), lambda i: (0, 0)),
            pl.BlockSpec((LOCAL, E), lambda i: (0, 0)),
            pl.BlockSpec((2, PAD, E), lambda i: (i, 0, 0)),
        ],
        out_specs=[
            pl.BlockSpec((1, 4, HALF, 256), lambda i: (i, 0, 0, 0)),
            pl.BlockSpec((1, 4, HALF, 256), lambda i: (i, 0, 0, 0)),
            pl.BlockSpec((3, ZN, ROWS), lambda i: (0, 0, 0)),
        ],
        out_shape=[shape(4, 4, HALF, 256)] * 2 + [shape(3, ZN, ROWS)],
        compiler_params=params(12),
        cost_estimate=pl.CostEstimate(flops=3 * 2**30, bytes_accessed=10 * 2**20, transcendentals=2**21),
        name="forward",
    )(pos, xh, xl, q)


def block(i, pos_ref, lse_ref, side, q_ref):
    qh, ql = split(query_rows(q_ref))
    lse = cat([lse_ref[side, pl.ds(2 * i, 1), :], lse_ref[side, pl.ds(2 * i + 1, 1), :]], 1)
    return cat([qh, ql, qh], 0), local_labels(pos_ref, q_ref), lse


def delta(s, lse, rows, lab, at):
    p = jnp.exp(s - lse)
    return split(jnp.where(rows == lab - at, p - 1.0, p))


def gradients(g_acc, x, s, operands, first, count, tiles):
    qcat, lab, lse = operands
    rows = lax.broadcasted_iota(jnp.int32, (HALF, 256), 0)
    o = jnp.zeros((256, E), f32)
    for t in tiles:
        at = slice(t * HALF, (t + 1) * HALF)
        dh, dl = delta(s[t // 4][0, t % 4], lse, rows, lab, t * HALF)
        if first <= t < first + count:
            g_acc[t - first] += dot(cat([dh, dh, dl], 1), qcat, NN)
        if x is not None:
            o += dot(cat([dh, dh, dl], 0), cat([x[0][at], x[1][at], x[0][at]], 0), TN)
    return o * (E**-0.5)


def backward_a_kernel(pos_ref, part, xh, xl, mine, other, lse_ref, sm1, so0, so1, oo, up, down, token, g_acc):
    i = pl.program_id(0)

    @pl.when(i == 0)
    def _():
        g_acc[...] = jnp.zeros_like(g_acc)
        token[0] = 0.0

    @pl.when(i < 4)
    def _():
        operands = block(i, pos_ref, lse_ref, 0, mine)
        gradients(g_acc, None, (None, sm1), operands, 4, 4, range(4, 8))

    @pl.when(i >= 4)
    def _():
        operands = block(i - 4, pos_ref, lse_ref, 1, other)
        o = gradients(g_acc, (xh, xl), (so0, so1), operands, 4, 4, range(8))
        oo[0], oo[1] = o[:ROWS], o[ROWS:]

    @pl.when(i == ZN - 1)
    def _():
        for d in range(4):
            up[d * CUT : (d + 1) * CUT, :] = g_acc[d, :CUT, :]
            down[d * CUT : (d + 1) * CUT, :] = g_acc[d, CUT:, :]
        up[4 * CUT :, :] = down[4 * CUT :, :] = jnp.full((8, E), part[0], f32)


def backward_b_kernel(pos_ref, token, xh, xl, mine, other, lse_ref, sm0, sm1, so0, got, om, g_ref):
    i = pl.program_id(0)

    @pl.when(i == 0)
    def _():
        g_ref[...] = jnp.zeros_like(g_ref)

    @pl.when(i < 4)
    def _():
        operands = block(i, pos_ref, lse_ref, 1, other)
        gradients(g_ref, None, (so0, None), operands, 0, 4, range(4))

    @pl.when(i >= 4)
    def _():
        operands = block(i - 4, pos_ref, lse_ref, 0, mine)
        o = gradients(g_ref, (xh, xl), (sm0, sm1), operands, 0, 4, range(8))
        om[0], om[1] = o[:ROWS] + got[0], o[ROWS:] + got[1]


def whole(*dims):
    return pl.BlockSpec(dims, lambda i: (0,) * len(dims))


def early(*dims):
    return pl.BlockSpec(dims, lambda i: (jnp.minimum(i, 3),) + (0,) * (len(dims) - 1))


def late(*dims):
    return pl.BlockSpec(dims, lambda i: (jnp.maximum(i, 4) - 4,) + (0,) * (len(dims) - 1))


X_SPEC = whole(LOCAL, E)
Q = (2, PAD, E)
S = (1, 4, HALF, 256)


def backward_a(pos, part, xh, xl, mine, other, lse, *s):
    return pl.pallas_call(
        backward_a_kernel,
        grid=(ZN,),
        in_specs=[SMEM, SMEM, X_SPEC, X_SPEC, early(*Q), late(*Q), whole(2, ZN, ROWS)]
        + [early(*S), late(*S), late(*S)],
        out_specs=[late(2, ROWS, E)] + [whole(4 * CUT + 8, E)] * 2 + [SMEM],
        out_shape=[shape(ZN, ROWS, E)] + [shape(4 * CUT + 8, E)] * 2 + [shape(1)],
        scratch_shapes=[pltpu.VMEM((4, HALF, E), f32)],
        compiler_params=params(14),
        cost_estimate=pl.CostEstimate(flops=6 * 2**30, bytes_accessed=16 * 2**20, transcendentals=3 * 2**20),
        name="backward_a",
    )(pos, part, xh, xl, mine, other, lse, *s)


def backward_b(pos, token, xh, xl, mine, other, lse, *s):
    return pl.pallas_call(
        backward_b_kernel,
        grid=(ZN,),
        in_specs=[SMEM, SMEM, X_SPEC, X_SPEC, late(*Q), early(*Q), whole(2, ZN, ROWS)]
        + [late(*S), late(*S), early(*S), late(2, ROWS, E)],
        out_specs=[late(2, ROWS, E), whole(4, HALF, E)],
        out_shape=[shape(ZN, ROWS, E), shape(4, HALF, E)],
        compiler_params=params(14),
        cost_estimate=pl.CostEstimate(flops=6 * 2**30, bytes_accessed=16 * 2**20, transcendentals=3 * 2**20),
        name="backward_b",
    )(pos, token, xh, xl, mine, other, lse, *s)


def gather(qs, own):
    mine = lax.all_to_all(qs, "z", 0, 0, tiled=True)
    y0, x3, x1 = flip(own, 32), send(own, dx=1), send(own, dx=-1)
    y0, x3, x1 = lax.optimization_barrier((y0, x3, x1))
    y3, y1, x2 = send(y0, dx=1), send(y0, dx=-1), send(x3, dx=1)
    y3, y1, x2 = lax.optimization_barrier((y3, y1, x2))
    y2 = send(y1, dx=-1)
    return mine, [own, x1, x2, x3, y0, y1, y2, y3]


def fold_kernel(part, g, a, b, o, held, *out):
    held[...] = o[...]
    for d in range(4):
        at = slice(d * CUT, (d + 1) * CUT)
        out[d][:CUT] = g[d, :CUT] + a[at]
        out[d][CUT:HALF] = g[d, CUT:] + b[at]
        out[d][HALF : HALF + 1] = jnp.full((1, E), part[0], f32)
        out[d][HALF + 1 : HALF + 2] = a[4 * CUT : 4 * CUT + 1]
        out[d][HALF + 2 : HALF + 3] = b[4 * CUT : 4 * CUT + 1]
        out[d][HALF + 3 :] = jnp.zeros((5, E), f32)


def land_kernel(m0, m1, m2, m3, out):
    out[...] = (m0[...] + m2[...]) + (m1[...] + m3[...])


def join_kernel(pos_ref, mine, mine2, other, other2, out, loss):
    c = pos_ref[1]
    out[pl.ds(pl.multiple_of(c * HALF, HALF), HALF), :] = mine[:HALF] + mine2[:HALF]
    out[pl.ds(pl.multiple_of((1 - c) * HALF, HALF), HALF), :] = other[:HALF] + other2[:HALF]
    total = (mine[HALF : HALF + 1] + mine2[HALF : HALF + 1]) + (
        mine[HALF + 1 : HALF + 2] + mine[HALF + 2 : HALF + 3]
    )
    loss[0] = jnp.max(total) / 32768


def sum_kernel(got, out):
    total = got[0]
    for k in range(1, ZN):
        total += got[k]
    out[...] = total


def body(queries, items, labels):
    core, y_lo, x_at, z_at = (lax.axis_index(a) for a in ("c", "yl", "x", "z"))
    pos = jnp.stack([z_at, core, y_lo, x_at]).astype(jnp.int32)
    qs, own = small(
        start_kernel, [pos, queries, labels.reshape(1, ROWS), items], [shape(ZN, PAD, E), shape(HALF, E)]
    )
    mine, parts = gather(qs, own)
    xh, xl, mine = small(
        pack_items_kernel, parts + [mine], [shape(LOCAL, E, dtype=bf16)] * 2 + [shape(ZN, PAD, E)]
    )
    other = send(mine, dc=1)
    sm0, sm1, stat_m = forward(pos, xh, xl, mine)
    so0, so1, stat_o = forward(pos, xh, xl, other)
    (stats,) = small(spread_kernel, [stat_m, stat_o], [shape(2 * ZN, 2, 3, ZN, ROWS)])
    stats = lax.all_to_all(stats, ("c", "z"), 0, 0, tiled=True)
    lse, part = small(merge_kernel, [pos, stats], [shape(2, ZN, ROWS), shape(1)])
    oo, up, down, first = backward_a(pos, part, xh, xl, mine, other, lse, sm1, so0, so1)
    a, b = send(up, dy=1), send(down, dy=-1)
    o, g = backward_b(pos, first, xh, xl, mine, other, lse, sm0, sm1, so0, send(oo, dc=1))
    o, m0, m1, m2, m3 = small(fold_kernel, [part, g, a, b, o], [shape(ZN, ROWS, E)] + [shape(HALF + 8, E)] * 4)
    o = lax.all_to_all(o, "z", 0, 0, tiled=True)
    m2, m1, m3 = send(m2, dx=2), send(m1, dx=1), send(m3, dx=-1)
    (own,) = small(land_kernel, [m0, m1, m2, m3], [shape(HALF + 8, E)])
    got = send(own, dy=2)
    near = send(own, dc=1)
    item_grad, loss = small(
        join_kernel, [pos, own, got, near, send(got, dc=1)], [shape(2 * HALF, E), shape(1)]
    )
    (query_grad,) = small(sum_kernel, [o], [shape(ROWS, E)])
    return loss.reshape(()), query_grad, item_grad


def solution(mesh):
    grid = Mesh(mesh.devices.reshape(2, 2, 2, 4, 8), AXES)
    corpus = ("yl", "x", "z")
    in_specs = (P(AXES, None), P(corpus, None), P(AXES))
    out_specs = (P(), P(AXES, None), P(corpus, None))
    return jax.shard_map(body, mesh=grid, in_specs=in_specs, out_specs=out_specs, check_vma=False)
```

```python
import jax
import jax.numpy as jnp
from jax import lax
from jax.experimental import pallas as pl
from jax.experimental.pallas import tpu as pltpu
from jax.sharding import Mesh, PartitionSpec as P

E = 256
ZN, XN, YN = 8, 4, 4
ROWS = 128
PAD = 136
HALF = 256
CUT = HALF // 2
PIECES = 8
LOCAL = PIECES * HALF
AXES = ("yh", "c", "yl", "x", "z")
f32, bf16 = jnp.float32, jnp.bfloat16


def place(i):
    return (i >> 7) & 1, (i >> 6) & 1, (i >> 5) & 1, (i >> 3) & 3, i & 7


def index(yh, c, yl, x, z):
    return yh * 128 + c * 64 + yl * 32 + x * 8 + z


def pairs(dx=0, dy=0, dz=0, dc=0):
    out = []
    for i in range(256):
        yh, c, yl, x, z = place(i)
        y = (yh * 2 + yl + dy) % YN
        out.append((i, index(y >> 1, (c + dc) % 2, y & 1, (x + dx) % XN, (z + dz) % ZN)))
    return out


def send(a, **shift):
    return lax.ppermute(a, AXES, pairs(**shift))


def twin(a, axis, hops=1):
    up, down = pairs(**{axis: hops}), pairs(**{axis: -hops})
    return lax.ppermute(a, AXES, [(down if (i >> 6) & 1 else up)[i] for i in range(256)])


def split(a):
    hi = a.astype(bf16)
    return hi, (a - hi.astype(f32)).astype(bf16)


def dot(a, b, dims):
    return lax.dot_general(a, b, (dims, ((), ())), preferred_element_type=f32)


def cat(parts, axis):
    return jnp.concatenate(parts, axis=axis)


NT = ((1,), (1,))
NN = ((1,), (0,))
TN = ((0,), (0,))
SMEM = pl.BlockSpec(memory_space=pltpu.SMEM)
VMEM = pl.BlockSpec(memory_space=pltpu.VMEM)


def shape(*dims, dtype=f32):
    return jax.ShapeDtypeStruct(dims, dtype)


def params(mib):
    return pltpu.CompilerParams(vmem_limit_bytes=mib * 2**20)


def local_labels(pos_ref, q_ref):
    lab = cat([q_ref[0, ROWS : ROWS + 1, :ROWS], q_ref[1, ROWS : ROWS + 1, :ROWS]], 1)
    lab = lab.astype(jnp.int32)
    z, c, yl, x = pos_ref[0], pos_ref[1], pos_ref[2], pos_ref[3]
    here = ((lab >> 9) & 7 == z) & ((lab >> 8) & 1 == c)
    piece = (((lab >> 14) ^ yl) & 1) * 4 + (((lab >> 12) & 3) - x & 3)
    return jnp.where(here, piece * HALF + (lab & 255), -1)


def query_rows(q_ref):
    return cat([q_ref[0, :ROWS, :], q_ref[1, :ROWS, :]], 0) * (E**-0.5)


def small(kernel, ins, outs, smem_out=()):
    return pl.pallas_call(
        kernel,
        in_specs=[SMEM if a.ndim == 1 else VMEM for a in ins],
        out_specs=[SMEM if len(o.shape) == 1 else VMEM for o in outs],
        out_shape=outs,
        compiler_params=params(10),
        name=kernel.__name__,
    )(*ins)


def at(start, n):
    return pl.ds(pl.multiple_of(start, 8), n)


def start_kernel(pos_ref, queries, labels, items, q, own):
    q[:ROWS, :] = queries[...]
    q[ROWS:, :ROWS] = jnp.broadcast_to(labels[...].astype(f32), (PAD - ROWS, ROWS))
    q[ROWS:, ROWS:] = jnp.zeros((PAD - ROWS, E - ROWS), f32)
    own[...] = items[at(pos_ref[1] * HALF, HALF), :]


def pair_kernel(pos_ref, mine, other, out):
    n, c = mine.shape[0], pos_ref[1]
    out[at(c * n, n), :] = mine[...]
    out[at((1 - c) * n, n), :] = other[...]


def part_kernel(pos_ref, both, *refs):
    *_, mine, other = refs
    n, c = mine.shape[0], pos_ref[1]
    mine[...] = both[at(c * n, n), :]
    other[...] = both[at((1 - c) * n, n), :]


def stack_kernel(a, b, c, out):
    for k, ref in enumerate((a, b, c)):
        out[k * HALF : (k + 1) * HALF, :] = ref[...]


def pack_queries_kernel(pos_ref, q, qo, q4, qo4, r1, r2, r3, s1, s2, s3, mine, other):
    z, c = pos_ref[0], pos_ref[1]
    mine[z], other[z] = q[...], qo[...]
    mine[(z + 4) & 7], other[(z + 4) & 7] = q4[...], qo4[...]
    for k, r, s in ((1, r1, s1), (2, r2, s2), (3, r3, s3)):
        step = k - 2 * c * k
        for ref, where in ((r, (z - step) & 7), (s, (z + step) & 7)):
            mine[where] = ref[at(c * PAD, PAD), :]
            other[where] = ref[at((1 - c) * PAD, PAD), :]


def pack_items_kernel(pos_ref, own, near, across, far, y_own, y_rest, xh, xl):
    c = pos_ref[1]

    def put(slot, rows):
        xh[at(slot * HALF, HALF), :], xl[at(slot * HALF, HALF), :] = split(rows)

    put(0, own[...])
    put(3 - 2 * c, near[...])
    put(1 + 2 * c, across[...])
    put(2, far[...])
    put(4, y_own[...])
    put(7 - 2 * c, y_rest[:HALF, :])
    put(5 + 2 * c, y_rest[HALF : 2 * HALF, :])
    put(6, y_rest[2 * HALF :, :])


def join_stats(a, b):
    best = jnp.maximum(a[0], b[0])
    return best, a[1] * jnp.exp(a[0] - best) + b[1] * jnp.exp(b[0] - best)


def spread_kernel(mine, got, out):
    best, total = join_stats(mine, got)
    for k in range(ZN):
        out[k, 0] = best
        out[k, 1] = total
        out[k, 2] = mine[2] + got[2]


def merge_kernel(got, out):
    best = got[0, 0]
    for k in range(1, ZN):
        best = jnp.maximum(best, got[k, 0])
    total = pick = jnp.zeros((ZN, ROWS), f32)
    for k in range(ZN):
        total += got[k, 1] * jnp.exp(got[k, 0] - best)
        pick += got[k, 2]
    lse = best + jnp.log(total)
    out[:ZN] = lse
    out[ZN:] = jnp.full((8, ROWS), jnp.sum(lse - pick), f32)


def line_loss(own, other):
    row = own[ZN : ZN + 1, :] + other[ZN : ZN + 1, :]
    return cat([row, row], 1)


def forward_kernel(pos_ref, xh, xl, q_ref, s0_ref, s1_ref, stat_ref):
    qh, ql = split(query_rows(q_ref))
    qcat = cat([qh, qh, ql], 1)
    lab = local_labels(pos_ref, q_ref)
    rows = lax.broadcasted_iota(jnp.int32, (HALF, 256), 0)
    top = total = None
    pick = jnp.zeros((8, 256), f32)
    for t in range(PIECES):
        at = slice(t * HALF, (t + 1) * HALF)
        s = dot(cat([xh[at], xl[at], xh[at]], 1), qcat, NT)
        (s0_ref, s1_ref)[t // 4][0, t % 4] = s
        pick += jnp.sum(jnp.where(rows == lab - t * HALF, s, 0.0).reshape(32, 8, 256), axis=0)
        s = s.reshape(32, 8, 256)
        best = jnp.max(s, axis=0)
        if top is None:
            total = jnp.sum(jnp.exp(s - best[None]), axis=0)
        else:
            best = jnp.maximum(top, best)
            total = total * jnp.exp(top - best) + jnp.sum(jnp.exp(s - best[None]), axis=0)
        top = best
    best = jnp.max(top, axis=0, keepdims=True)
    total = jnp.sum(total * jnp.exp(top - best), axis=0, keepdims=True)
    pick = jnp.sum(pick, axis=0, keepdims=True)
    for h in range(2):
        z = 2 * pl.program_id(0) + h
        at = slice(h * ROWS, (h + 1) * ROWS)
        stat_ref[0, pl.ds(z, 1), :] = best[:, at]
        stat_ref[1, pl.ds(z, 1), :] = total[:, at]
        stat_ref[2, pl.ds(z, 1), :] = pick[:, at]


def forward(pos, xh, xl, q):
    return pl.pallas_call(
        forward_kernel,
        grid=(4,),
        in_specs=[
            SMEM,
            pl.BlockSpec((LOCAL, E), lambda i: (0, 0)),
            pl.BlockSpec((LOCAL, E), lambda i: (0, 0)),
            pl.BlockSpec((2, PAD, E), lambda i: (i, 0, 0)),
        ],
        out_specs=[
            pl.BlockSpec((1, 4, HALF, 256), lambda i: (i, 0, 0, 0)),
            pl.BlockSpec((1, 4, HALF, 256), lambda i: (i, 0, 0, 0)),
            pl.BlockSpec((3, ZN, ROWS), lambda i: (0, 0, 0)),
        ],
        out_shape=[shape(4, 4, HALF, 256)] * 2 + [shape(3, ZN, ROWS)],
        compiler_params=params(12),
        cost_estimate=pl.CostEstimate(flops=3 * 2**30, bytes_accessed=10 * 2**20, transcendentals=2**21),
        name="forward",
    )(pos, xh, xl, q)


def block(i, pos_ref, lse_ref, q_ref):
    qh, ql = split(query_rows(q_ref))
    lse = cat([lse_ref[pl.ds(2 * i, 1), :], lse_ref[pl.ds(2 * i + 1, 1), :]], 1)
    return cat([qh, ql, qh], 0), local_labels(pos_ref, q_ref), lse


def delta(s, lse, rows, lab, at):
    p = jnp.exp(s - lse)
    return split(jnp.where(rows == lab - at, p - 1.0, p))


def gradients(g_acc, x, s, operands, first, count, tiles):
    qcat, lab, lse = operands
    rows = lax.broadcasted_iota(jnp.int32, (HALF, 256), 0)
    o = jnp.zeros((256, E), f32)
    for t in tiles:
        at = slice(t * HALF, (t + 1) * HALF)
        dh, dl = delta(s[t // 4][0, t % 4], lse, rows, lab, t * HALF)
        if first <= t < first + count:
            g_acc[t - first] += dot(cat([dh, dh, dl], 1), qcat, NN)
        if x is not None:
            o += dot(cat([dh, dh, dl], 0), cat([x[0][at], x[1][at], x[0][at]], 0), TN)
    return o * (E**-0.5)


def backward_a_kernel(pos_ref, xh, xl, mine, other, lse_m, lse_o, sm1, so0, so1, oo, up, down, token, g_acc):
    i = pl.program_id(0)

    @pl.when(i == 0)
    def _():
        g_acc[...] = jnp.zeros_like(g_acc)
        token[0] = 0.0

    @pl.when(i < 4)
    def _():
        operands = block(i, pos_ref, lse_m, mine)
        gradients(g_acc, None, (None, sm1), operands, 4, 4, range(4, 8))

    @pl.when(i >= 4)
    def _():
        operands = block(i - 4, pos_ref, lse_o, other)
        o = gradients(g_acc, (xh, xl), (so0, so1), operands, 4, 4, range(8))
        oo[0], oo[1] = o[:ROWS], o[ROWS:]

    @pl.when(i == ZN - 1)
    def _():
        for d in range(4):
            up[d * CUT : (d + 1) * CUT, :] = g_acc[d, :CUT, :]
            down[d * CUT : (d + 1) * CUT, :] = g_acc[d, CUT:, :]
        up[4 * CUT :, :] = down[4 * CUT :, :] = jnp.broadcast_to(line_loss(lse_m, lse_o), (8, E))


def backward_b_kernel(pos_ref, token, xh, xl, mine, other, lse_m, lse_o, sm0, sm1, so0, got, om, g_ref):
    i = pl.program_id(0)

    @pl.when(i == 0)
    def _():
        g_ref[...] = jnp.zeros_like(g_ref)

    @pl.when(i < 4)
    def _():
        operands = block(i, pos_ref, lse_o, other)
        gradients(g_ref, None, (so0, None), operands, 0, 4, range(4))

    @pl.when(i >= 4)
    def _():
        operands = block(i - 4, pos_ref, lse_m, mine)
        o = gradients(g_ref, (xh, xl), (sm0, sm1), operands, 0, 4, range(8))
        om[0], om[1] = o[:ROWS] + got[0], o[ROWS:] + got[1]


def whole(*dims):
    return pl.BlockSpec(dims, lambda i: (0,) * len(dims))


def early(*dims):
    return pl.BlockSpec(dims, lambda i: (jnp.minimum(i, 3),) + (0,) * (len(dims) - 1))


def late(*dims):
    return pl.BlockSpec(dims, lambda i: (jnp.maximum(i, 4) - 4,) + (0,) * (len(dims) - 1))


X_SPEC = whole(LOCAL, E)
LSE = whole(2 * ZN, ROWS)
Q = (2, PAD, E)
S = (1, 4, HALF, 256)


def backward_a(pos, *operands):
    return pl.pallas_call(
        backward_a_kernel,
        grid=(ZN,),
        in_specs=[SMEM, X_SPEC, X_SPEC, early(*Q), late(*Q), LSE, LSE]
        + [early(*S), late(*S), late(*S)],
        out_specs=[late(2, ROWS, E)] + [whole(4 * CUT + 8, E)] * 2 + [SMEM],
        out_shape=[shape(ZN, ROWS, E)] + [shape(4 * CUT + 8, E)] * 2 + [shape(1)],
        scratch_shapes=[pltpu.VMEM((4, HALF, E), f32)],
        compiler_params=params(14),
        cost_estimate=pl.CostEstimate(flops=6 * 2**30, bytes_accessed=16 * 2**20, transcendentals=3 * 2**20),
        name="backward_a",
    )(pos, *operands)


def backward_b(pos, *operands):
    return pl.pallas_call(
        backward_b_kernel,
        grid=(ZN,),
        in_specs=[SMEM, SMEM, X_SPEC, X_SPEC, late(*Q), early(*Q), LSE, LSE]
        + [late(*S), late(*S), early(*S), late(2, ROWS, E)],
        out_specs=[late(2, ROWS, E), whole(4, HALF, E)],
        out_shape=[shape(ZN, ROWS, E), shape(4, HALF, E)],
        compiler_params=params(14),
        cost_estimate=pl.CostEstimate(flops=6 * 2**30, bytes_accessed=16 * 2**20, transcendentals=3 * 2**20),
        name="backward_b",
    )(pos, *operands)


def gather(pos, q, own, items):
    chunk, two = shape(PAD, E), shape(2 * PAD, E)
    half = shape(HALF, E)
    x1 = twin(items, "dx")
    qo = send(q, dc=1)
    (r0,) = small(pair_kernel, [pos, q, qo], [two])
    r1 = twin(r0, "dz")
    r2 = twin(r0, "dz", 2)
    far = twin(own, "dx", 2)
    y0 = twin(own, "dy")
    near, rest = small(part_kernel, [pos, x1, y0, r2], [half, half])
    across = send(rest, dc=1)
    (rest,) = small(stack_kernel, [near, across, far], [shape(3 * HALF, E)])
    y_rest = twin(rest, "dy")
    r3 = twin(r2, "dz")
    s1, s2 = send(r1, dc=1), send(r2, dc=1)
    third, _ = small(part_kernel, [pos, r2, far], [chunk, chunk])
    q4 = twin(third, "dz", 2)
    s3 = send(r3, dc=1)
    mine, other = small(
        pack_queries_kernel, [pos, q, qo, q4, send(q4, dc=1), r1, r2, r3, s1, s2, s3], [shape(ZN, PAD, E)] * 2
    )
    xh, xl = small(
        pack_items_kernel, [pos, own, near, across, far, y0, y_rest], [shape(LOCAL, E, dtype=bf16)] * 2
    )
    return mine, other, xh, xl


def fold_kernel(lse_m, lse_o, g, a, b, o, held, *out):
    held[...] = o[...]
    for d in range(4):
        at = slice(d * CUT, (d + 1) * CUT)
        out[d][:CUT] = g[d, :CUT] + a[at]
        out[d][CUT:HALF] = g[d, CUT:] + b[at]
        out[d][HALF : HALF + 1] = line_loss(lse_m, lse_o)
        out[d][HALF + 1 : HALF + 2] = a[4 * CUT : 4 * CUT + 1]
        out[d][HALF + 2 : HALF + 3] = b[4 * CUT : 4 * CUT + 1]
        out[d][HALF + 3 :] = jnp.zeros((5, E), f32)


def land_kernel(m0, m1, m2, m3, out):
    out[...] = (m0[...] + m2[...]) + (m1[...] + m3[...])


def join_kernel(pos_ref, mine, mine2, other, other2, out, loss):
    c = pos_ref[1]
    out[pl.ds(pl.multiple_of(c * HALF, HALF), HALF), :] = mine[:HALF] + mine2[:HALF]
    out[pl.ds(pl.multiple_of((1 - c) * HALF, HALF), HALF), :] = other[:HALF] + other2[:HALF]
    total = (mine[HALF : HALF + 1] + mine2[HALF : HALF + 1]) + (
        mine[HALF + 1 : HALF + 2] + mine[HALF + 2 : HALF + 3]
    )
    loss[0] = jnp.max(total) / 32768


def sum_kernel(got, out):
    total = got[0]
    for k in range(1, ZN):
        total += got[k]
    out[...] = total


def body(queries, items, labels):
    core, y_lo, x_at, z_at = (lax.axis_index(a) for a in ("c", "yl", "x", "z"))
    pos = jnp.stack([z_at, core, y_lo, x_at]).astype(jnp.int32)
    q, own = small(
        start_kernel, [pos, queries, labels.reshape(1, ROWS), items], [shape(PAD, E), shape(HALF, E)]
    )
    mine, other, xh, xl = gather(pos, q, own, items)
    sm0, sm1, stat_m = forward(pos, xh, xl, mine)
    so0, so1, stat_o = forward(pos, xh, xl, other)
    (stats,) = small(spread_kernel, [stat_m, send(stat_o, dc=1)], [shape(ZN, 3, ZN, ROWS)])
    stats = lax.all_to_all(stats, "z", 0, 0, tiled=True)
    (lse,) = small(merge_kernel, [stats], [shape(2 * ZN, ROWS)])
    lse = [lse, send(lse, dc=1)]
    oo, up, down, first = backward_a(pos, xh, xl, mine, other, *lse, sm1, so0, so1)
    a, b = send(up, dy=1), send(down, dy=-1)
    o, g = backward_b(pos, first, xh, xl, mine, other, *lse, sm0, sm1, so0, send(oo, dc=1))
    o, m0, m1, m2, m3 = small(fold_kernel, [*lse, g, a, b, o], [shape(ZN, ROWS, E)] + [shape(HALF + 8, E)] * 4)
    o = lax.all_to_all(o, "z", 0, 0, tiled=True)
    m2, m1, m3 = send(m2, dx=2), send(m1, dx=1), send(m3, dx=-1)
    (own,) = small(land_kernel, [m0, m1, m2, m3], [shape(HALF + 8, E)])
    got = send(own, dy=2)
    near = send(own, dc=1)
    item_grad, loss = small(
        join_kernel, [pos, own, got, near, send(got, dc=1)], [shape(2 * HALF, E), shape(1)]
    )
    (query_grad,) = small(sum_kernel, [o], [shape(ROWS, E)])
    return loss.reshape(()), query_grad, item_grad


def solution(mesh):
    grid = Mesh(mesh.devices.reshape(2, 2, 2, 4, 8), AXES)
    corpus = ("yl", "x", "z")
    in_specs = (P(AXES, None), P(corpus, None), P(AXES))
    out_specs = (P(), P(AXES, None), P(corpus, None))
    return jax.shard_map(body, mesh=grid, in_specs=in_specs, out_specs=out_specs, check_vma=False)
```

```python
import jax
import jax.numpy as jnp
from jax import lax
from jax.experimental import pallas as pl
from jax.experimental.pallas import tpu as pltpu
from jax.sharding import Mesh, PartitionSpec as P

E = 256
ZN, XN, YN = 8, 4, 4
ROWS = 128
PAD = 136
HALF = 256
CUT = HALF // 2
PIECES = 8
LOCAL = PIECES * HALF
AXES = ("yh", "c", "yl", "x", "z")
f32, bf16 = jnp.float32, jnp.bfloat16


def place(i):
    return (i >> 7) & 1, (i >> 6) & 1, (i >> 5) & 1, (i >> 3) & 3, i & 7


def index(yh, c, yl, x, z):
    return yh * 128 + c * 64 + yl * 32 + x * 8 + z


def pairs(dx=0, dy=0, dz=0, dc=0):
    out = []
    for i in range(256):
        yh, c, yl, x, z = place(i)
        y = (yh * 2 + yl + dy) % YN
        out.append((i, index(y >> 1, (c + dc) % 2, y & 1, (x + dx) % XN, (z + dz) % ZN)))
    return out


def send(a, **shift):
    return lax.ppermute(a, AXES, pairs(**shift))


def twin(a, axis, hops=1):
    up, down = pairs(**{axis: hops}), pairs(**{axis: -hops})
    return lax.ppermute(a, AXES, [(down if (i >> 6) & 1 else up)[i] for i in range(256)])


def split(a):
    hi = a.astype(bf16)
    return hi, (a - hi.astype(f32)).astype(bf16)


def dot(a, b, dims):
    return lax.dot_general(a, b, (dims, ((), ())), preferred_element_type=f32)


def cat(parts, axis):
    return jnp.concatenate(parts, axis=axis)


NT = ((1,), (1,))
NN = ((1,), (0,))
TN = ((0,), (0,))
SMEM = pl.BlockSpec(memory_space=pltpu.SMEM)
VMEM = pl.BlockSpec(memory_space=pltpu.VMEM)


def shape(*dims, dtype=f32):
    return jax.ShapeDtypeStruct(dims, dtype)


def params(mib):
    return pltpu.CompilerParams(vmem_limit_bytes=mib * 2**20)


def local_labels(pos_ref, q_ref):
    lab = cat([q_ref[0, ROWS : ROWS + 1, :ROWS], q_ref[1, ROWS : ROWS + 1, :ROWS]], 1)
    lab = lab.astype(jnp.int32)
    z, c, yl, x = pos_ref[0], pos_ref[1], pos_ref[2], pos_ref[3]
    here = ((lab >> 9) & 7 == z) & ((lab >> 8) & 1 == c)
    piece = (((lab >> 14) ^ yl) & 1) * 4 + (((lab >> 12) & 3) - x & 3)
    return jnp.where(here, piece * HALF + (lab & 255), -1)


def query_rows(q_ref):
    return cat([q_ref[0, :ROWS, :], q_ref[1, :ROWS, :]], 0) * (E**-0.5)


def small(kernel, ins, outs, smem_out=()):
    return pl.pallas_call(
        kernel,
        in_specs=[SMEM if a.ndim == 1 else VMEM for a in ins],
        out_specs=[SMEM if len(o.shape) == 1 else VMEM for o in outs],
        out_shape=outs,
        compiler_params=params(10),
        name=kernel.__name__,
    )(*ins)


def at(start, n):
    return pl.ds(pl.multiple_of(start, 8), n)


def start_kernel(pos_ref, queries, labels, items, q, own):
    q[:ROWS, :] = queries[...]
    q[ROWS:, :ROWS] = jnp.broadcast_to(labels[...].astype(f32), (PAD - ROWS, ROWS))
    q[ROWS:, ROWS:] = jnp.zeros((PAD - ROWS, E - ROWS), f32)
    own[...] = items[at(pos_ref[1] * HALF, HALF), :]


def pair_kernel(pos_ref, mine, other, out):
    n, c = mine.shape[0], pos_ref[1]
    out[at(c * n, n), :] = mine[...]
    out[at((1 - c) * n, n), :] = other[...]


def part_kernel(pos_ref, both, *refs):
    *_, mine, other = refs
    n, c = mine.shape[0], pos_ref[1]
    mine[...] = both[at(c * n, n), :]
    other[...] = both[at((1 - c) * n, n), :]


def stack_kernel(*refs):
    *parts, out = refs
    row = 0
    for ref in parts:
        n = ref.shape[0]
        out[row : row + n, :] = ref[...]
        row += n


def pack_queries_kernel(pos_ref, q, qo, r2, r314, s2, s314, mine, other):
    z, c = pos_ref[0], pos_ref[1]
    mine[z], other[z] = q[...], qo[...]
    mine[(z + 4) & 7], other[(z + 4) & 7] = r314[4 * PAD :, :], s314[4 * PAD :, :]
    for k, r, s, row in ((2, r2, s2, 0), (3, r314, s314, 0), (1, r314, s314, 2 * PAD)):
        step = k - 2 * c * k
        for ref, where in ((r, (z - step) & 7), (s, (z + step) & 7)):
            mine[where] = ref[at(row + c * PAD, PAD), :]
            other[where] = ref[at(row + (1 - c) * PAD, PAD), :]


def pack_items_kernel(pos_ref, own, near, across, far, y_own, y_rest, xh, xl):
    c = pos_ref[1]

    def put(slot, rows):
        xh[at(slot * HALF, HALF), :], xl[at(slot * HALF, HALF), :] = split(rows)

    put(0, own[...])
    put(3 - 2 * c, near[...])
    put(1 + 2 * c, across[...])
    put(2, far[...])
    put(4, y_own[...])
    put(7 - 2 * c, y_rest[:HALF, :])
    put(5 + 2 * c, y_rest[HALF : 2 * HALF, :])
    put(6, y_rest[2 * HALF :, :])


def join_stats(a, b):
    best = jnp.maximum(a[0], b[0])
    return best, a[1] * jnp.exp(a[0] - best) + b[1] * jnp.exp(b[0] - best)


def spread_kernel(mine, got, out):
    best, total = join_stats(mine, got)
    for k in range(ZN):
        out[k, 0] = best
        out[k, 1] = total
        out[k, 2] = mine[2] + got[2]


def merge_kernel(got, out):
    best = got[0, 0]
    for k in range(1, ZN):
        best = jnp.maximum(best, got[k, 0])
    total = pick = jnp.zeros((ZN, ROWS), f32)
    for k in range(ZN):
        total += got[k, 1] * jnp.exp(got[k, 0] - best)
        pick += got[k, 2]
    lse = best + jnp.log(total)
    out[:ZN] = lse
    out[ZN:] = jnp.full((8, ROWS), jnp.sum(lse - pick), f32)


def line_loss(own, other):
    row = own[ZN : ZN + 1, :] + other[ZN : ZN + 1, :]
    return cat([row, row], 1)


def forward_kernel(pos_ref, xh, xl, q_ref, s0_ref, s1_ref, stat_ref):
    qh, ql = split(query_rows(q_ref))
    qcat = cat([qh, qh, ql], 1)
    lab = local_labels(pos_ref, q_ref)
    rows = lax.broadcasted_iota(jnp.int32, (HALF, 256), 0)
    top = total = None
    pick = jnp.zeros((8, 256), f32)
    for t in range(PIECES):
        at = slice(t * HALF, (t + 1) * HALF)
        s = dot(cat([xh[at], xl[at], xh[at]], 1), qcat, NT)
        (s0_ref, s1_ref)[t // 4][0, t % 4] = s
        pick += jnp.sum(jnp.where(rows == lab - t * HALF, s, 0.0).reshape(32, 8, 256), axis=0)
        s = s.reshape(32, 8, 256)
        best = jnp.max(s, axis=0)
        if top is None:
            total = jnp.sum(jnp.exp(s - best[None]), axis=0)
        else:
            best = jnp.maximum(top, best)
            total = total * jnp.exp(top - best) + jnp.sum(jnp.exp(s - best[None]), axis=0)
        top = best
    best = jnp.max(top, axis=0, keepdims=True)
    total = jnp.sum(total * jnp.exp(top - best), axis=0, keepdims=True)
    pick = jnp.sum(pick, axis=0, keepdims=True)
    for h in range(2):
        z = 2 * pl.program_id(0) + h
        at = slice(h * ROWS, (h + 1) * ROWS)
        stat_ref[0, pl.ds(z, 1), :] = best[:, at]
        stat_ref[1, pl.ds(z, 1), :] = total[:, at]
        stat_ref[2, pl.ds(z, 1), :] = pick[:, at]


def forward(pos, xh, xl, q):
    return pl.pallas_call(
        forward_kernel,
        grid=(4,),
        in_specs=[
            SMEM,
            pl.BlockSpec((LOCAL, E), lambda i: (0, 0)),
            pl.BlockSpec((LOCAL, E), lambda i: (0, 0)),
            pl.BlockSpec((2, PAD, E), lambda i: (i, 0, 0)),
        ],
        out_specs=[
            pl.BlockSpec((1, 4, HALF, 256), lambda i: (i, 0, 0, 0)),
            pl.BlockSpec((1, 4, HALF, 256), lambda i: (i, 0, 0, 0)),
            pl.BlockSpec((3, ZN, ROWS), lambda i: (0, 0, 0)),
        ],
        out_shape=[shape(4, 4, HALF, 256)] * 2 + [shape(3, ZN, ROWS)],
        compiler_params=params(12),
        cost_estimate=pl.CostEstimate(flops=3 * 2**30, bytes_accessed=10 * 2**20, transcendentals=2**21),
        name="forward",
    )(pos, xh, xl, q)


def block(i, pos_ref, lse_ref, q_ref):
    qh, ql = split(query_rows(q_ref))
    lse = cat([lse_ref[pl.ds(2 * i, 1), :], lse_ref[pl.ds(2 * i + 1, 1), :]], 1)
    return cat([qh, ql, qh], 0), local_labels(pos_ref, q_ref), lse


def delta(s, lse, rows, lab, at):
    p = jnp.exp(s - lse)
    return split(jnp.where(rows == lab - at, p - 1.0, p))


def gradients(g_acc, x, s, operands, first, count, tiles):
    qcat, lab, lse = operands
    rows = lax.broadcasted_iota(jnp.int32, (HALF, 256), 0)
    o = jnp.zeros((256, E), f32)
    for t in tiles:
        at = slice(t * HALF, (t + 1) * HALF)
        dh, dl = delta(s[t // 4][0, t % 4], lse, rows, lab, t * HALF)
        if first <= t < first + count:
            g_acc[t - first] += dot(cat([dh, dh, dl], 1), qcat, NN)
        if x is not None:
            o += dot(cat([dh, dh, dl], 0), cat([x[0][at], x[1][at], x[0][at]], 0), TN)
    return o * (E**-0.5)


def backward_a_kernel(pos_ref, xh, xl, mine, other, lse_m, lse_o, sm1, so0, so1, oo, up, down, token, g_acc):
    i = pl.program_id(0)

    @pl.when(i == 0)
    def _():
        g_acc[...] = jnp.zeros_like(g_acc)
        token[0] = 0.0

    @pl.when(i < 4)
    def _():
        operands = block(i, pos_ref, lse_m, mine)
        gradients(g_acc, None, (None, sm1), operands, 4, 4, range(4, 8))

    @pl.when(i >= 4)
    def _():
        operands = block(i - 4, pos_ref, lse_o, other)
        o = gradients(g_acc, (xh, xl), (so0, so1), operands, 4, 4, range(8))
        oo[0], oo[1] = o[:ROWS], o[ROWS:]

    @pl.when(i == ZN - 1)
    def _():
        for d in range(4):
            up[d * CUT : (d + 1) * CUT, :] = g_acc[d, :CUT, :]
            down[d * CUT : (d + 1) * CUT, :] = g_acc[d, CUT:, :]
        up[4 * CUT :, :] = down[4 * CUT :, :] = jnp.broadcast_to(line_loss(lse_m, lse_o), (8, E))


def backward_b_kernel(pos_ref, token, xh, xl, mine, other, lse_m, lse_o, sm0, sm1, so0, got, om, g_ref):
    i = pl.program_id(0)

    @pl.when(i == 0)
    def _():
        g_ref[...] = jnp.zeros_like(g_ref)

    @pl.when(i < 4)
    def _():
        operands = block(i, pos_ref, lse_o, other)
        gradients(g_ref, None, (so0, None), operands, 0, 4, range(4))

    @pl.when(i >= 4)
    def _():
        operands = block(i - 4, pos_ref, lse_m, mine)
        o = gradients(g_ref, (xh, xl), (sm0, sm1), operands, 0, 4, range(8))
        om[0], om[1] = o[:ROWS] + got[0], o[ROWS:] + got[1]


def whole(*dims):
    return pl.BlockSpec(dims, lambda i: (0,) * len(dims))


def early(*dims):
    return pl.BlockSpec(dims, lambda i: (jnp.minimum(i, 3),) + (0,) * (len(dims) - 1))


def late(*dims):
    return pl.BlockSpec(dims, lambda i: (jnp.maximum(i, 4) - 4,) + (0,) * (len(dims) - 1))


X_SPEC = whole(LOCAL, E)
LSE = whole(2 * ZN, ROWS)
Q = (2, PAD, E)
S = (1, 4, HALF, 256)


def backward_a(pos, *operands):
    return pl.pallas_call(
        backward_a_kernel,
        grid=(ZN,),
        in_specs=[SMEM, X_SPEC, X_SPEC, early(*Q), late(*Q), LSE, LSE]
        + [early(*S), late(*S), late(*S)],
        out_specs=[late(2, ROWS, E)] + [whole(4 * CUT + 8, E)] * 2 + [SMEM],
        out_shape=[shape(ZN, ROWS, E)] + [shape(4 * CUT + 8, E)] * 2 + [shape(1)],
        scratch_shapes=[pltpu.VMEM((4, HALF, E), f32)],
        compiler_params=params(14),
        cost_estimate=pl.CostEstimate(flops=6 * 2**30, bytes_accessed=16 * 2**20, transcendentals=3 * 2**20),
        name="backward_a",
    )(pos, *operands)


def backward_b(pos, *operands):
    return pl.pallas_call(
        backward_b_kernel,
        grid=(ZN,),
        in_specs=[SMEM, SMEM, X_SPEC, X_SPEC, late(*Q), early(*Q), LSE, LSE]
        + [late(*S), late(*S), early(*S), late(2, ROWS, E)],
        out_specs=[late(2, ROWS, E), whole(4, HALF, E)],
        out_shape=[shape(ZN, ROWS, E), shape(4, HALF, E)],
        compiler_params=params(14),
        cost_estimate=pl.CostEstimate(flops=6 * 2**30, bytes_accessed=16 * 2**20, transcendentals=3 * 2**20),
        name="backward_b",
    )(pos, *operands)


def gather(pos, q, own, items):
    chunk, two = shape(PAD, E), shape(2 * PAD, E)
    half = shape(HALF, E)
    x1 = twin(items, "dx")
    qo = send(q, dc=1)
    (r0,) = small(pair_kernel, [pos, q, qo], [two])
    r2 = twin(r0, "dz", 2)
    far = twin(own, "dx", 2)
    y0 = twin(own, "dy")
    third, _ = small(part_kernel, [pos, r2, y0, far], [chunk, chunk])
    (r20,) = small(stack_kernel, [r2, r0], [shape(4 * PAD, E)])
    r31, q4 = twin(r20, "dz"), twin(third, "dz", 2)
    near, rest = small(part_kernel, [pos, x1, third], [half, half])
    across = send(rest, dc=1)
    (rest,) = small(stack_kernel, [near, across, far], [shape(3 * HALF, E)])
    y_rest = twin(rest, "dy")
    (r314,) = small(stack_kernel, [r31, q4], [shape(5 * PAD, E)])
    mine, other = small(
        pack_queries_kernel,
        [pos, q, qo, r2, r314, send(r2, dc=1), send(r314, dc=1)],
        [shape(ZN, PAD, E)] * 2,
    )
    xh, xl = small(
        pack_items_kernel, [pos, own, near, across, far, y0, y_rest], [shape(LOCAL, E, dtype=bf16)] * 2
    )
    return mine, other, xh, xl


def fold_kernel(lse_m, lse_o, g, a, b, o, held, *out):
    for d in range(4):
        at = slice(d * CUT, (d + 1) * CUT)
        out[d][:CUT] = g[d, :CUT] + a[at]
        out[d][CUT:HALF] = g[d, CUT:] + b[at]
        out[d][HALF : HALF + 1] = line_loss(lse_m, lse_o)
        out[d][HALF + 1 : HALF + 2] = a[4 * CUT : 4 * CUT + 1]
        out[d][HALF + 2 : HALF + 3] = b[4 * CUT : 4 * CUT + 1]
        out[d][HALF + 3 :] = jnp.zeros((5, E), f32)


def fold(*operands):
    anywhere = pl.BlockSpec(memory_space=pl.ANY)
    return pl.pallas_call(
        fold_kernel,
        in_specs=[VMEM] * 5 + [anywhere],
        out_specs=[anywhere] + [VMEM] * 4,
        out_shape=[shape(ZN, ROWS, E)] + [shape(HALF + 8, E)] * 4,
        input_output_aliases={5: 0},
        compiler_params=params(10),
        name="fold",
    )(*operands)


def land_kernel(m0, m1, m2, m3, out):
    out[...] = (m0[...] + m2[...]) + (m1[...] + m3[...])


def join_kernel(pos_ref, mine, mine2, other, other2, out, loss):
    c = pos_ref[1]
    out[pl.ds(pl.multiple_of(c * HALF, HALF), HALF), :] = mine[:HALF] + mine2[:HALF]
    out[pl.ds(pl.multiple_of((1 - c) * HALF, HALF), HALF), :] = other[:HALF] + other2[:HALF]
    total = (mine[HALF : HALF + 1] + mine2[HALF : HALF + 1]) + (
        mine[HALF + 1 : HALF + 2] + mine[HALF + 2 : HALF + 3]
    )
    loss[0] = jnp.max(total) / 32768


def sum_kernel(got, out):
    total = got[0]
    for k in range(1, ZN):
        total += got[k]
    out[...] = total


def body(queries, items, labels):
    core, y_lo, x_at, z_at = (lax.axis_index(a) for a in ("c", "yl", "x", "z"))
    pos = jnp.stack([z_at, core, y_lo, x_at]).astype(jnp.int32)
    q, own = small(
        start_kernel, [pos, queries, labels.reshape(1, ROWS), items], [shape(PAD, E), shape(HALF, E)]
    )
    mine, other, xh, xl = gather(pos, q, own, items)
    sm0, sm1, stat_m = forward(pos, xh, xl, mine)
    so0, so1, stat_o = forward(pos, xh, xl, other)
    (stats,) = small(spread_kernel, [stat_m, send(stat_o, dc=1)], [shape(ZN, 3, ZN, ROWS)])
    stats = lax.all_to_all(stats, "z", 0, 0, tiled=True)
    (lse,) = small(merge_kernel, [stats], [shape(2 * ZN, ROWS)])
    lse = [lse, send(lse, dc=1)]
    oo, up, down, first = backward_a(pos, xh, xl, mine, other, *lse, sm1, so0, so1)
    a, b = send(up, dy=1), send(down, dy=-1)
    o, g = backward_b(pos, first, xh, xl, mine, other, *lse, sm0, sm1, so0, send(oo, dc=1))
    o, m0, m1, m2, m3 = fold(*lse, g, a, b, o)
    o = lax.all_to_all(o, "z", 0, 0, tiled=True)
    m2, m1, m3 = send(m2, dx=2), send(m1, dx=1), send(m3, dx=-1)
    (own,) = small(land_kernel, [m0, m1, m2, m3], [shape(HALF + 8, E)])
    got = send(own, dy=2)
    near = send(own, dc=1)
    item_grad, loss = small(
        join_kernel, [pos, own, got, near, send(got, dc=1)], [shape(2 * HALF, E), shape(1)]
    )
    (query_grad,) = small(sum_kernel, [o], [shape(ROWS, E)])
    return loss.reshape(()), query_grad, item_grad


def solution(mesh):
    grid = Mesh(mesh.devices.reshape(2, 2, 2, 4, 8), AXES)
    corpus = ("yl", "x", "z")
    in_specs = (P(AXES, None), P(corpus, None), P(AXES))
    out_specs = (P(), P(AXES, None), P(corpus, None))
    return jax.shard_map(body, mesh=grid, in_specs=in_specs, out_specs=out_specs, check_vma=False)
```

```python
import jax
import jax.numpy as jnp
from jax import lax
from jax.experimental import pallas as pl
from jax.experimental.pallas import tpu as pltpu
from jax.sharding import Mesh, PartitionSpec as P

E = 256
ZN, XN, YN = 8, 4, 4
ROWS = 128
PAD = 136
HALF = 256
CUT = HALF // 2
N = 4
W = N * ROWS
STEPS = 8 // N
PIECES = 8
LOCAL = PIECES * HALF
AXES = ("yh", "c", "yl", "x", "z")
f32, bf16 = jnp.float32, jnp.bfloat16


def place(i):
    return (i >> 7) & 1, (i >> 6) & 1, (i >> 5) & 1, (i >> 3) & 3, i & 7


def index(yh, c, yl, x, z):
    return yh * 128 + c * 64 + yl * 32 + x * 8 + z


def pairs(dx=0, dy=0, dz=0, dc=0):
    out = []
    for i in range(256):
        yh, c, yl, x, z = place(i)
        y = (yh * 2 + yl + dy) % YN
        out.append((i, index(y >> 1, (c + dc) % 2, y & 1, (x + dx) % XN, (z + dz) % ZN)))
    return out


def send(a, **shift):
    return lax.ppermute(a, AXES, pairs(**shift))


def twin(a, axis, hops=1):
    up, down = pairs(**{axis: hops}), pairs(**{axis: -hops})
    return lax.ppermute(a, AXES, [(down if (i >> 6) & 1 else up)[i] for i in range(256)])


def split(a):
    hi = a.astype(bf16)
    return hi, (a - hi.astype(f32)).astype(bf16)


def dot(a, b, dims):
    return lax.dot_general(a, b, (dims, ((), ())), preferred_element_type=f32)


def cat(parts, axis):
    return jnp.concatenate(parts, axis=axis)


NT = ((1,), (1,))
NN = ((1,), (0,))
TN = ((0,), (0,))
SMEM = pl.BlockSpec(memory_space=pltpu.SMEM)
VMEM = pl.BlockSpec(memory_space=pltpu.VMEM)


def shape(*dims, dtype=f32):
    return jax.ShapeDtypeStruct(dims, dtype)


def params(mib):
    return pltpu.CompilerParams(vmem_limit_bytes=mib * 2**20)


def local_labels(pos_ref, q_ref):
    lab = cat([q_ref[k, ROWS : ROWS + 1, :ROWS] for k in range(N)], 1)
    lab = lab.astype(jnp.int32)
    z, c, yl, x = pos_ref[0], pos_ref[1], pos_ref[2], pos_ref[3]
    here = ((lab >> 9) & 7 == z) & ((lab >> 8) & 1 == c)
    piece = (((lab >> 14) ^ yl) & 1) * 4 + (((lab >> 12) & 3) - x & 3)
    return jnp.where(here, piece * HALF + (lab & 255), -1)


def query_rows(q_ref):
    return cat([q_ref[k, :ROWS, :] for k in range(N)], 0) * (E**-0.5)


def small(kernel, ins, outs, smem_out=()):
    return pl.pallas_call(
        kernel,
        in_specs=[SMEM if a.ndim == 1 else VMEM for a in ins],
        out_specs=[SMEM if len(o.shape) == 1 else VMEM for o in outs],
        out_shape=outs,
        compiler_params=params(10),
        name=kernel.__name__,
    )(*ins)


def at(start, n):
    return pl.ds(pl.multiple_of(start, 8), n)


def start_kernel(pos_ref, queries, labels, items, q, own):
    q[:ROWS, :] = queries[...]
    q[ROWS:, :ROWS] = jnp.broadcast_to(labels[...].astype(f32), (PAD - ROWS, ROWS))
    q[ROWS:, ROWS:] = jnp.zeros((PAD - ROWS, E - ROWS), f32)
    own[...] = items[at(pos_ref[1] * HALF, HALF), :]


def pair_kernel(pos_ref, mine, other, out):
    n, c = mine.shape[0], pos_ref[1]
    out[at(c * n, n), :] = mine[...]
    out[at((1 - c) * n, n), :] = other[...]


def part_kernel(pos_ref, both, *refs):
    *_, mine, other = refs
    n, c = mine.shape[0], pos_ref[1]
    mine[...] = both[at(c * n, n), :]
    other[...] = both[at((1 - c) * n, n), :]


def stack_kernel(*refs):
    *parts, out = refs
    row = 0
    for ref in parts:
        n = ref.shape[0]
        out[row : row + n, :] = ref[...]
        row += n


def pack_queries_kernel(pos_ref, q, qo, r2, r314, s2, s314, mine, other):
    z, c = pos_ref[0], pos_ref[1]
    mine[z], other[z] = q[...], qo[...]
    mine[(z + 4) & 7], other[(z + 4) & 7] = r314[4 * PAD :, :], s314[4 * PAD :, :]
    for k, r, s, row in ((2, r2, s2, 0), (3, r314, s314, 0), (1, r314, s314, 2 * PAD)):
        step = k - 2 * c * k
        for ref, where in ((r, (z - step) & 7), (s, (z + step) & 7)):
            mine[where] = ref[at(row + c * PAD, PAD), :]
            other[where] = ref[at(row + (1 - c) * PAD, PAD), :]


def pack_items_kernel(pos_ref, own, near, across, far, y_own, y_rest, xh, xl):
    c = pos_ref[1]

    def put(slot, rows):
        xh[at(slot * HALF, HALF), :], xl[at(slot * HALF, HALF), :] = split(rows)

    put(0, own[...])
    put(3 - 2 * c, near[...])
    put(1 + 2 * c, across[...])
    put(2, far[...])
    put(4, y_own[...])
    put(7 - 2 * c, y_rest[:HALF, :])
    put(5 + 2 * c, y_rest[HALF : 2 * HALF, :])
    put(6, y_rest[2 * HALF :, :])


def join_stats(a, b):
    best = jnp.maximum(a[0], b[0])
    return best, a[1] * jnp.exp(a[0] - best) + b[1] * jnp.exp(b[0] - best)


def spread_kernel(mine, got, out):
    best, total = join_stats(mine, got)
    for k in range(ZN):
        out[k, 0] = best
        out[k, 1] = total
        out[k, 2] = mine[2] + got[2]


def merge_kernel(got, out):
    best = got[0, 0]
    for k in range(1, ZN):
        best = jnp.maximum(best, got[k, 0])
    total = pick = jnp.zeros((ZN, ROWS), f32)
    for k in range(ZN):
        total += got[k, 1] * jnp.exp(got[k, 0] - best)
        pick += got[k, 2]
    lse = best + jnp.log(total)
    out[:ZN] = lse
    out[ZN:] = jnp.full((8, ROWS), jnp.sum(lse - pick), f32)


def line_loss(own, other):
    row = own[ZN : ZN + 1, :] + other[ZN : ZN + 1, :]
    return cat([row, row], 1)


def forward_kernel(pos_ref, xh, xl, q_ref, s0_ref, s1_ref, stat_ref):
    qh, ql = split(query_rows(q_ref))
    qcat = cat([qh, qh, ql], 1)
    lab = local_labels(pos_ref, q_ref)
    rows = lax.broadcasted_iota(jnp.int32, (HALF, W), 0)
    top = total = None
    pick = jnp.zeros((8, W), f32)
    for t in range(PIECES):
        at = slice(t * HALF, (t + 1) * HALF)
        s = dot(cat([xh[at], xl[at], xh[at]], 1), qcat, NT)
        (s0_ref, s1_ref)[t // 4][0, t % 4] = s
        pick += jnp.sum(jnp.where(rows == lab - t * HALF, s, 0.0).reshape(32, 8, W), axis=0)
        s = s.reshape(32, 8, W)
        best = jnp.max(s, axis=0)
        if top is None:
            total = jnp.sum(jnp.exp(s - best[None]), axis=0)
        else:
            best = jnp.maximum(top, best)
            total = total * jnp.exp(top - best) + jnp.sum(jnp.exp(s - best[None]), axis=0)
        top = best
    best = jnp.max(top, axis=0, keepdims=True)
    total = jnp.sum(total * jnp.exp(top - best), axis=0, keepdims=True)
    pick = jnp.sum(pick, axis=0, keepdims=True)
    for h in range(N):
        z = N * pl.program_id(0) + h
        at = slice(h * ROWS, (h + 1) * ROWS)
        stat_ref[0, pl.ds(z, 1), :] = best[:, at]
        stat_ref[1, pl.ds(z, 1), :] = total[:, at]
        stat_ref[2, pl.ds(z, 1), :] = pick[:, at]


def forward(pos, xh, xl, q):
    return pl.pallas_call(
        forward_kernel,
        grid=(STEPS,),
        in_specs=[
            SMEM,
            pl.BlockSpec((LOCAL, E), lambda i: (0, 0)),
            pl.BlockSpec((LOCAL, E), lambda i: (0, 0)),
            pl.BlockSpec((N, PAD, E), lambda i: (i, 0, 0)),
        ],
        out_specs=[
            pl.BlockSpec((1, 4, HALF, W), lambda i: (i, 0, 0, 0)),
            pl.BlockSpec((1, 4, HALF, W), lambda i: (i, 0, 0, 0)),
            pl.BlockSpec((3, ZN, ROWS), lambda i: (0, 0, 0)),
        ],
        out_shape=[shape(STEPS, 4, HALF, W)] * 2 + [shape(3, ZN, ROWS)],
        compiler_params=params(18),
        cost_estimate=pl.CostEstimate(flops=3 * 2**30, bytes_accessed=10 * 2**20, transcendentals=2**21),
        name="forward",
    )(pos, xh, xl, q)


def block(i, pos_ref, lse_ref, q_ref):
    qh, ql = split(query_rows(q_ref))
    lse = cat([lse_ref[pl.ds(N * i + k, 1), :] for k in range(N)], 1)
    return cat([qh, ql, qh], 0), local_labels(pos_ref, q_ref), lse


def delta(s, lse, rows, lab, at):
    p = jnp.exp(s - lse)
    return split(jnp.where(rows == lab - at, p - 1.0, p))


def gradients(g_acc, x, s, operands, first, count, tiles):
    qcat, lab, lse = operands
    rows = lax.broadcasted_iota(jnp.int32, (HALF, W), 0)
    o = jnp.zeros((W, E), f32)
    for t in tiles:
        at = slice(t * HALF, (t + 1) * HALF)
        dh, dl = delta(s[t // 4][0, t % 4], lse, rows, lab, t * HALF)
        if first <= t < first + count:
            g_acc[t - first] += dot(cat([dh, dh, dl], 1), qcat, NN)
        if x is not None:
            o += dot(cat([dh, dh, dl], 0), cat([x[0][at], x[1][at], x[0][at]], 0), TN)
    return o * (E**-0.5)


def backward_a_kernel(pos_ref, xh, xl, mine, other, lse_m, lse_o, sm1, so0, so1, oo, up, down, token, g_acc):
    i = pl.program_id(0)

    @pl.when(i == 0)
    def _():
        g_acc[...] = jnp.zeros_like(g_acc)
        token[0] = 0.0

    @pl.when(i < STEPS)
    def _():
        operands = block(i, pos_ref, lse_m, mine)
        gradients(g_acc, None, (None, sm1), operands, 4, 4, range(4, 8))

    @pl.when(i >= STEPS)
    def _():
        operands = block(i - STEPS, pos_ref, lse_o, other)
        o = gradients(g_acc, (xh, xl), (so0, so1), operands, 4, 4, range(8))
        for k in range(N):
            oo[k] = o[k * ROWS : (k + 1) * ROWS]

    @pl.when(i == 2 * STEPS - 1)
    def _():
        for d in range(4):
            up[d * CUT : (d + 1) * CUT, :] = g_acc[d, :CUT, :]
            down[d * CUT : (d + 1) * CUT, :] = g_acc[d, CUT:, :]
        up[4 * CUT :, :] = down[4 * CUT :, :] = jnp.broadcast_to(line_loss(lse_m, lse_o), (8, E))


def backward_b_kernel(pos_ref, token, xh, xl, mine, other, lse_m, lse_o, sm0, sm1, so0, got, om, g_ref):
    i = pl.program_id(0)

    @pl.when(i == 0)
    def _():
        g_ref[...] = jnp.zeros_like(g_ref)

    @pl.when(i < STEPS)
    def _():
        operands = block(i, pos_ref, lse_o, other)
        gradients(g_ref, None, (so0, None), operands, 0, 4, range(4))

    @pl.when(i >= STEPS)
    def _():
        operands = block(i - STEPS, pos_ref, lse_m, mine)
        o = gradients(g_ref, (xh, xl), (sm0, sm1), operands, 0, 4, range(8))
        for k in range(N):
            om[k] = o[k * ROWS : (k + 1) * ROWS] + got[k]


def whole(*dims):
    return pl.BlockSpec(dims, lambda i: (0,) * len(dims))


def early(*dims):
    return pl.BlockSpec(dims, lambda i: (jnp.minimum(i, STEPS - 1),) + (0,) * (len(dims) - 1))


def late(*dims):
    return pl.BlockSpec(dims, lambda i: (jnp.maximum(i, STEPS) - STEPS,) + (0,) * (len(dims) - 1))


X_SPEC = whole(LOCAL, E)
LSE = whole(2 * ZN, ROWS)
Q = (N, PAD, E)
S = (1, 4, HALF, W)


def backward_a(pos, *operands):
    return pl.pallas_call(
        backward_a_kernel,
        grid=(2 * STEPS,),
        in_specs=[SMEM, X_SPEC, X_SPEC, early(*Q), late(*Q), LSE, LSE]
        + [early(*S), late(*S), late(*S)],
        out_specs=[late(N, ROWS, E)] + [whole(4 * CUT + 8, E)] * 2 + [SMEM],
        out_shape=[shape(ZN, ROWS, E)] + [shape(4 * CUT + 8, E)] * 2 + [shape(1)],
        scratch_shapes=[pltpu.VMEM((4, HALF, E), f32)],
        compiler_params=params(24),
        cost_estimate=pl.CostEstimate(flops=6 * 2**30, bytes_accessed=16 * 2**20, transcendentals=3 * 2**20),
        name="backward_a",
    )(pos, *operands)


def backward_b(pos, *operands):
    return pl.pallas_call(
        backward_b_kernel,
        grid=(2 * STEPS,),
        in_specs=[SMEM, SMEM, X_SPEC, X_SPEC, late(*Q), early(*Q), LSE, LSE]
        + [late(*S), late(*S), early(*S), late(N, ROWS, E)],
        out_specs=[late(N, ROWS, E), whole(4, HALF, E)],
        out_shape=[shape(ZN, ROWS, E), shape(4, HALF, E)],
        compiler_params=params(24),
        cost_estimate=pl.CostEstimate(flops=6 * 2**30, bytes_accessed=16 * 2**20, transcendentals=3 * 2**20),
        name="backward_b",
    )(pos, *operands)


def gather(pos, q, own, items):
    chunk, two = shape(PAD, E), shape(2 * PAD, E)
    half = shape(HALF, E)
    x1 = twin(items, "dx")
    qo = send(q, dc=1)
    (r0,) = small(pair_kernel, [pos, q, qo], [two])
    r2 = twin(r0, "dz", 2)
    far = twin(own, "dx", 2)
    y0 = twin(own, "dy")
    third, _ = small(part_kernel, [pos, r2, y0, far], [chunk, chunk])
    (r20,) = small(stack_kernel, [r2, r0], [shape(4 * PAD, E)])
    r31, q4 = twin(r20, "dz"), twin(third, "dz", 2)
    near, rest = small(part_kernel, [pos, x1, third], [half, half])
    across = send(rest, dc=1)
    (rest,) = small(stack_kernel, [near, across, far], [shape(3 * HALF, E)])
    y_rest = twin(rest, "dy")
    (r314,) = small(stack_kernel, [r31, q4], [shape(5 * PAD, E)])
    mine, other = small(
        pack_queries_kernel,
        [pos, q, qo, r2, r314, send(r2, dc=1), send(r314, dc=1)],
        [shape(ZN, PAD, E)] * 2,
    )
    xh, xl = small(
        pack_items_kernel, [pos, own, near, across, far, y0, y_rest], [shape(LOCAL, E, dtype=bf16)] * 2
    )
    return mine, other, xh, xl


def fold_kernel(lse_m, lse_o, g, a, b, o, held, *out):
    for d in range(4):
        at = slice(d * CUT, (d + 1) * CUT)
        out[d][:CUT] = g[d, :CUT] + a[at]
        out[d][CUT:HALF] = g[d, CUT:] + b[at]
        out[d][HALF : HALF + 1] = line_loss(lse_m, lse_o)
        out[d][HALF + 1 : HALF + 2] = a[4 * CUT : 4 * CUT + 1]
        out[d][HALF + 2 : HALF + 3] = b[4 * CUT : 4 * CUT + 1]
        out[d][HALF + 3 :] = jnp.zeros((5, E), f32)


def fold(*operands):
    anywhere = pl.BlockSpec(memory_space=pl.ANY)
    return pl.pallas_call(
        fold_kernel,
        in_specs=[VMEM] * 5 + [anywhere],
        out_specs=[anywhere] + [VMEM] * 4,
        out_shape=[shape(ZN, ROWS, E)] + [shape(HALF + 8, E)] * 4,
        input_output_aliases={5: 0},
        compiler_params=params(10),
        name="fold",
    )(*operands)


def land_kernel(m0, m1, m2, m3, out):
    out[...] = (m0[...] + m2[...]) + (m1[...] + m3[...])


def join_kernel(pos_ref, mine, mine2, other, other2, out, loss):
    c = pos_ref[1]
    out[pl.ds(pl.multiple_of(c * HALF, HALF), HALF), :] = mine[:HALF] + mine2[:HALF]
    out[pl.ds(pl.multiple_of((1 - c) * HALF, HALF), HALF), :] = other[:HALF] + other2[:HALF]
    total = (mine[HALF : HALF + 1] + mine2[HALF : HALF + 1]) + (
        mine[HALF + 1 : HALF + 2] + mine[HALF + 2 : HALF + 3]
    )
    loss[0] = jnp.max(total) / 32768


def sum_kernel(got, out):
    total = got[0]
    for k in range(1, ZN):
        total += got[k]
    out[...] = total


def body(queries, items, labels):
    core, y_lo, x_at, z_at = (lax.axis_index(a) for a in ("c", "yl", "x", "z"))
    pos = jnp.stack([z_at, core, y_lo, x_at]).astype(jnp.int32)
    q, own = small(
        start_kernel, [pos, queries, labels.reshape(1, ROWS), items], [shape(PAD, E), shape(HALF, E)]
    )
    mine, other, xh, xl = gather(pos, q, own, items)
    sm0, sm1, stat_m = forward(pos, xh, xl, mine)
    so0, so1, stat_o = forward(pos, xh, xl, other)
    (stats,) = small(spread_kernel, [stat_m, send(stat_o, dc=1)], [shape(ZN, 3, ZN, ROWS)])
    stats = lax.all_to_all(stats, "z", 0, 0, tiled=True)
    (lse,) = small(merge_kernel, [stats], [shape(2 * ZN, ROWS)])
    lse = [lse, send(lse, dc=1)]
    oo, up, down, first = backward_a(pos, xh, xl, mine, other, *lse, sm1, so0, so1)
    a, b = send(up, dy=1), send(down, dy=-1)
    o, g = backward_b(pos, first, xh, xl, mine, other, *lse, sm0, sm1, so0, send(oo, dc=1))
    o, m0, m1, m2, m3 = fold(*lse, g, a, b, o)
    o = lax.all_to_all(o, "z", 0, 0, tiled=True)
    m2, m1, m3 = send(m2, dx=2), send(m1, dx=1), send(m3, dx=-1)
    (own,) = small(land_kernel, [m0, m1, m2, m3], [shape(HALF + 8, E)])
    got = send(own, dy=2)
    near = send(own, dc=1)
    item_grad, loss = small(
        join_kernel, [pos, own, got, near, send(got, dc=1)], [shape(2 * HALF, E), shape(1)]
    )
    (query_grad,) = small(sum_kernel, [o], [shape(ROWS, E)])
    return loss.reshape(()), query_grad, item_grad


def solution(mesh):
    grid = Mesh(mesh.devices.reshape(2, 2, 2, 4, 8), AXES)
    corpus = ("yl", "x", "z")
    in_specs = (P(AXES, None), P(corpus, None), P(AXES))
    out_specs = (P(), P(AXES, None), P(corpus, None))
    return jax.shard_map(body, mesh=grid, in_specs=in_specs, out_specs=out_specs, check_vma=False)
```

```python
import jax
import jax.numpy as jnp
from jax import lax
from jax.experimental import pallas as pl
from jax.experimental.pallas import tpu as pltpu
from jax.sharding import Mesh, PartitionSpec as P

E = 256
ZN, XN, YN = 8, 4, 4
ROWS = 128
PAD = 136
HALF = 256
CUT = HALF // 2
N = 4
W = N * ROWS
STEPS = 8 // N
PIECES = 8
LOCAL = PIECES * HALF
AXES = ("yh", "c", "yl", "x", "z")
f32, bf16 = jnp.float32, jnp.bfloat16


def place(i):
    return (i >> 7) & 1, (i >> 6) & 1, (i >> 5) & 1, (i >> 3) & 3, i & 7


def index(yh, c, yl, x, z):
    return yh * 128 + c * 64 + yl * 32 + x * 8 + z


def pairs(dx=0, dy=0, dz=0, dc=0):
    out = []
    for i in range(256):
        yh, c, yl, x, z = place(i)
        y = (yh * 2 + yl + dy) % YN
        out.append((i, index(y >> 1, (c + dc) % 2, y & 1, (x + dx) % XN, (z + dz) % ZN)))
    return out


def send(a, **shift):
    return lax.ppermute(a, AXES, pairs(**shift))


def twin(a, axis, hops=1):
    up, down = pairs(**{axis: hops}), pairs(**{axis: -hops})
    return lax.ppermute(a, AXES, [(down if (i >> 6) & 1 else up)[i] for i in range(256)])


def split(a):
    hi = a.astype(bf16)
    return hi, (a - hi.astype(f32)).astype(bf16)


def dot(a, b, dims):
    return lax.dot_general(a, b, (dims, ((), ())), preferred_element_type=f32)


def cat(parts, axis):
    return jnp.concatenate(parts, axis=axis)


NT = ((1,), (1,))
NN = ((1,), (0,))
TN = ((0,), (0,))
SMEM = pl.BlockSpec(memory_space=pltpu.SMEM)
VMEM = pl.BlockSpec(memory_space=pltpu.VMEM)


def shape(*dims, dtype=f32):
    return jax.ShapeDtypeStruct(dims, dtype)


def params(mib):
    return pltpu.CompilerParams(vmem_limit_bytes=mib * 2**20)


def local_labels(pos_ref, q_ref):
    lab = cat([q_ref[k, ROWS : ROWS + 1, :ROWS] for k in range(N)], 1)
    lab = lab.astype(jnp.int32)
    z, c, yl, x = pos_ref[0], pos_ref[1], pos_ref[2], pos_ref[3]
    here = ((lab >> 9) & 7 == z) & ((lab >> 8) & 1 == c)
    piece = (((lab >> 14) ^ yl) & 1) * 4 + (((lab >> 12) & 3) - x & 3)
    return jnp.where(here, piece * HALF + (lab & 255), -1)


def query_rows(q_ref):
    return cat([q_ref[k, :ROWS, :] for k in range(N)], 0) * (E**-0.5)


def small(kernel, ins, outs, smem_out=()):
    return pl.pallas_call(
        kernel,
        in_specs=[SMEM if a.ndim == 1 else VMEM for a in ins],
        out_specs=[SMEM if len(o.shape) == 1 else VMEM for o in outs],
        out_shape=outs,
        compiler_params=params(10),
        name=kernel.__name__,
    )(*ins)


def at(start, n):
    return pl.ds(pl.multiple_of(start, 8), n)


def start_kernel(queries, labels, q):
    q[:ROWS, :] = queries[...]
    q[ROWS:, :ROWS] = jnp.broadcast_to(labels[...].astype(f32), (PAD - ROWS, ROWS))
    q[ROWS:, ROWS:] = jnp.zeros((PAD - ROWS, E - ROWS), f32)


def own_kernel(pos_ref, items, own):
    own[...] = items[at(pos_ref[1] * HALF, HALF), :]


def pair_kernel(pos_ref, mine, other, out):
    n, c = mine.shape[0], pos_ref[1]
    out[at(c * n, n), :] = mine[...]
    out[at((1 - c) * n, n), :] = other[...]


def part_kernel(pos_ref, both, *refs):
    *_, mine, other = refs
    n, c = mine.shape[0], pos_ref[1]
    mine[...] = both[at(c * n, n), :]
    other[...] = both[at((1 - c) * n, n), :]


def third_kernel(pos_ref, both, after, after2, mine):
    mine[...] = both[at(pos_ref[1] * PAD, PAD), :]


def cut_third(*operands):
    anywhere = pl.BlockSpec(memory_space=pl.ANY)
    return pl.pallas_call(
        third_kernel,
        in_specs=[SMEM, VMEM, anywhere, anywhere],
        out_specs=VMEM,
        out_shape=shape(PAD, E),
        compiler_params=params(10),
        name="third",
    )(*operands)


def stack_kernel(*refs):
    *parts, out = refs
    row = 0
    for ref in parts:
        n = ref.shape[0]
        out[row : row + n, :] = ref[...]
        row += n


def pack_queries_kernel(pos_ref, q, qo, r2, r314, s2, s314, mine, other):
    z, c = pos_ref[0], pos_ref[1]
    mine[z], other[z] = q[...], qo[...]
    mine[(z + 4) & 7], other[(z + 4) & 7] = r314[4 * PAD :, :], s314[4 * PAD :, :]
    for k, r, s, row in ((2, r2, s2, 0), (3, r314, s314, 0), (1, r314, s314, 2 * PAD)):
        step = k - 2 * c * k
        for ref, where in ((r, (z - step) & 7), (s, (z + step) & 7)):
            mine[where] = ref[at(row + c * PAD, PAD), :]
            other[where] = ref[at(row + (1 - c) * PAD, PAD), :]


def pack_items_kernel(pos_ref, own, near, across, far, y_own, y_rest, xh, xl):
    c = pos_ref[1]

    def put(slot, rows):
        xh[at(slot * HALF, HALF), :], xl[at(slot * HALF, HALF), :] = split(rows)

    put(0, own[...])
    put(3 - 2 * c, near[...])
    put(1 + 2 * c, across[...])
    put(2, far[...])
    put(4, y_own[...])
    put(7 - 2 * c, y_rest[:HALF, :])
    put(5 + 2 * c, y_rest[HALF : 2 * HALF, :])
    put(6, y_rest[2 * HALF :, :])


def join_stats(a, b):
    best = jnp.maximum(a[0], b[0])
    return best, a[1] * jnp.exp(a[0] - best) + b[1] * jnp.exp(b[0] - best)


def spread_kernel(mine, got, out):
    best, total = join_stats(mine, got)
    for k in range(ZN):
        out[k, 0] = best
        out[k, 1] = total
        out[k, 2] = mine[2] + got[2]


def merge_kernel(got, out):
    best = got[0, 0]
    for k in range(1, ZN):
        best = jnp.maximum(best, got[k, 0])
    total = pick = jnp.zeros((ZN, ROWS), f32)
    for k in range(ZN):
        total += got[k, 1] * jnp.exp(got[k, 0] - best)
        pick += got[k, 2]
    lse = best + jnp.log(total)
    out[:ZN] = lse
    out[ZN:] = jnp.full((8, ROWS), jnp.sum(lse - pick), f32)


def line_loss(own, other):
    row = own[ZN : ZN + 1, :] + other[ZN : ZN + 1, :]
    return cat([row, row], 1)


def forward_kernel(pos_ref, xh, xl, q_ref, s0_ref, s1_ref, stat_ref):
    qh, ql = split(query_rows(q_ref))
    qcat = cat([qh, qh, ql], 1)
    lab = local_labels(pos_ref, q_ref)
    rows = lax.broadcasted_iota(jnp.int32, (HALF, W), 0)
    top = total = None
    pick = jnp.zeros((8, W), f32)
    for t in range(PIECES):
        at = slice(t * HALF, (t + 1) * HALF)
        s = dot(cat([xh[at], xl[at], xh[at]], 1), qcat, NT)
        (s0_ref, s1_ref)[t // 4][0, t % 4] = s
        pick += jnp.sum(jnp.where(rows == lab - t * HALF, s, 0.0).reshape(32, 8, W), axis=0)
        s = s.reshape(32, 8, W)
        best = jnp.max(s, axis=0)
        if top is None:
            total = jnp.sum(jnp.exp(s - best[None]), axis=0)
        else:
            best = jnp.maximum(top, best)
            total = total * jnp.exp(top - best) + jnp.sum(jnp.exp(s - best[None]), axis=0)
        top = best
    best = jnp.max(top, axis=0, keepdims=True)
    total = jnp.sum(total * jnp.exp(top - best), axis=0, keepdims=True)
    pick = jnp.sum(pick, axis=0, keepdims=True)
    for h in range(N):
        z = N * pl.program_id(0) + h
        at = slice(h * ROWS, (h + 1) * ROWS)
        stat_ref[0, pl.ds(z, 1), :] = best[:, at]
        stat_ref[1, pl.ds(z, 1), :] = total[:, at]
        stat_ref[2, pl.ds(z, 1), :] = pick[:, at]


def forward(pos, xh, xl, q):
    return pl.pallas_call(
        forward_kernel,
        grid=(STEPS,),
        in_specs=[
            SMEM,
            pl.BlockSpec((LOCAL, E), lambda i: (0, 0)),
            pl.BlockSpec((LOCAL, E), lambda i: (0, 0)),
            pl.BlockSpec((N, PAD, E), lambda i: (i, 0, 0)),
        ],
        out_specs=[
            pl.BlockSpec((1, 4, HALF, W), lambda i: (i, 0, 0, 0)),
            pl.BlockSpec((1, 4, HALF, W), lambda i: (i, 0, 0, 0)),
            pl.BlockSpec((3, ZN, ROWS), lambda i: (0, 0, 0)),
        ],
        out_shape=[shape(STEPS, 4, HALF, W)] * 2 + [shape(3, ZN, ROWS)],
        compiler_params=params(18),
        cost_estimate=pl.CostEstimate(flops=3 * 2**30, bytes_accessed=10 * 2**20, transcendentals=2**21),
        name="forward",
    )(pos, xh, xl, q)


def block(i, pos_ref, lse_ref, q_ref):
    qh, ql = split(query_rows(q_ref))
    lse = cat([lse_ref[pl.ds(N * i + k, 1), :] for k in range(N)], 1)
    return cat([qh, ql, qh], 0), local_labels(pos_ref, q_ref), lse


def delta(s, lse, rows, lab, at):
    p = jnp.exp(s - lse)
    return split(jnp.where(rows == lab - at, p - 1.0, p))


def gradients(g_acc, x, s, operands, first, count, tiles):
    qcat, lab, lse = operands
    rows = lax.broadcasted_iota(jnp.int32, (HALF, W), 0)
    o = jnp.zeros((W, E), f32)
    for t in tiles:
        at = slice(t * HALF, (t + 1) * HALF)
        dh, dl = delta(s[t // 4][0, t % 4], lse, rows, lab, t * HALF)
        if first <= t < first + count:
            g_acc[t - first] += dot(cat([dh, dh, dl], 1), qcat, NN)
        if x is not None:
            o += dot(cat([dh, dh, dl], 0), cat([x[0][at], x[1][at], x[0][at]], 0), TN)
    return o * (E**-0.5)


def backward_a_kernel(pos_ref, xh, xl, mine, other, lse_m, lse_o, sm1, so0, so1, oo, up, down, token, g_acc):
    i = pl.program_id(0)

    @pl.when(i == 0)
    def _():
        g_acc[...] = jnp.zeros_like(g_acc)
        token[0] = 0.0

    @pl.when(i < STEPS)
    def _():
        operands = block(i, pos_ref, lse_m, mine)
        gradients(g_acc, None, (None, sm1), operands, 4, 4, range(4, 8))

    @pl.when(i >= STEPS)
    def _():
        operands = block(i - STEPS, pos_ref, lse_o, other)
        o = gradients(g_acc, (xh, xl), (so0, so1), operands, 4, 4, range(8))
        for k in range(N):
            oo[k] = o[k * ROWS : (k + 1) * ROWS]

    @pl.when(i == 2 * STEPS - 1)
    def _():
        for d in range(4):
            up[d * CUT : (d + 1) * CUT, :] = g_acc[d, :CUT, :]
            down[d * CUT : (d + 1) * CUT, :] = g_acc[d, CUT:, :]
        up[4 * CUT :, :] = down[4 * CUT :, :] = jnp.broadcast_to(line_loss(lse_m, lse_o), (8, E))


def backward_b_kernel(pos_ref, token, xh, xl, mine, other, lse_m, lse_o, sm0, sm1, so0, got, om, g_ref):
    i = pl.program_id(0)

    @pl.when(i == 0)
    def _():
        g_ref[...] = jnp.zeros_like(g_ref)

    @pl.when(i < STEPS)
    def _():
        operands = block(i, pos_ref, lse_o, other)
        gradients(g_ref, None, (so0, None), operands, 0, 4, range(4))

    @pl.when(i >= STEPS)
    def _():
        operands = block(i - STEPS, pos_ref, lse_m, mine)
        o = gradients(g_ref, (xh, xl), (sm0, sm1), operands, 0, 4, range(8))
        for k in range(N):
            om[k] = o[k * ROWS : (k + 1) * ROWS] + got[k]


def whole(*dims):
    return pl.BlockSpec(dims, lambda i: (0,) * len(dims))


def early(*dims):
    return pl.BlockSpec(dims, lambda i: (jnp.minimum(i, STEPS - 1),) + (0,) * (len(dims) - 1))


def late(*dims):
    return pl.BlockSpec(dims, lambda i: (jnp.maximum(i, STEPS) - STEPS,) + (0,) * (len(dims) - 1))


X_SPEC = whole(LOCAL, E)
LSE = whole(2 * ZN, ROWS)
Q = (N, PAD, E)
S = (1, 4, HALF, W)


def backward_a(pos, *operands):
    return pl.pallas_call(
        backward_a_kernel,
        grid=(2 * STEPS,),
        in_specs=[SMEM, X_SPEC, X_SPEC, early(*Q), late(*Q), LSE, LSE]
        + [early(*S), late(*S), late(*S)],
        out_specs=[late(N, ROWS, E)] + [whole(4 * CUT + 8, E)] * 2 + [SMEM],
        out_shape=[shape(ZN, ROWS, E)] + [shape(4 * CUT + 8, E)] * 2 + [shape(1)],
        scratch_shapes=[pltpu.VMEM((4, HALF, E), f32)],
        compiler_params=params(24),
        cost_estimate=pl.CostEstimate(flops=6 * 2**30, bytes_accessed=16 * 2**20, transcendentals=3 * 2**20),
        name="backward_a",
    )(pos, *operands)


def backward_b(pos, *operands):
    return pl.pallas_call(
        backward_b_kernel,
        grid=(2 * STEPS,),
        in_specs=[SMEM, SMEM, X_SPEC, X_SPEC, late(*Q), early(*Q), LSE, LSE]
        + [late(*S), late(*S), early(*S), late(N, ROWS, E)],
        out_specs=[late(N, ROWS, E), whole(4, HALF, E)],
        out_shape=[shape(ZN, ROWS, E), shape(4, HALF, E)],
        compiler_params=params(24),
        cost_estimate=pl.CostEstimate(flops=6 * 2**30, bytes_accessed=16 * 2**20, transcendentals=3 * 2**20),
        name="backward_b",
    )(pos, *operands)


def gather(pos, q, own, items):
    two = shape(2 * PAD, E)
    half = shape(HALF, E)
    x1 = twin(items, "dx")
    qo = send(q, dc=1)
    (r0,) = small(pair_kernel, [pos, q, qo], [two])
    r2 = twin(r0, "dz", 2)
    far = twin(own, "dx", 2)
    y0 = twin(own, "dy")
    third = cut_third(pos, r2, y0, far)
    (r20,) = small(stack_kernel, [r2, r0], [shape(4 * PAD, E)])
    r31, q4 = twin(r20, "dz"), twin(third, "dz", 2)
    near, rest = small(part_kernel, [pos, x1, third], [half, half])
    across = send(rest, dc=1)
    (rest,) = small(stack_kernel, [near, across, far], [shape(3 * HALF, E)])
    y_rest = twin(rest, "dy")
    (r314,) = small(stack_kernel, [r31, q4], [shape(5 * PAD, E)])
    mine, other = small(
        pack_queries_kernel,
        [pos, q, qo, r2, r314, send(r2, dc=1), send(r314, dc=1)],
        [shape(ZN, PAD, E)] * 2,
    )
    xh, xl = small(
        pack_items_kernel, [pos, own, near, across, far, y0, y_rest], [shape(LOCAL, E, dtype=bf16)] * 2
    )
    return mine, other, xh, xl


def fold_kernel(lse_m, lse_o, g, a, b, o, held, *out):
    for d in range(4):
        at = slice(d * CUT, (d + 1) * CUT)
        out[d][:CUT] = g[d, :CUT] + a[at]
        out[d][CUT:HALF] = g[d, CUT:] + b[at]
        out[d][HALF : HALF + 1] = line_loss(lse_m, lse_o)
        out[d][HALF + 1 : HALF + 2] = a[4 * CUT : 4 * CUT + 1]
        out[d][HALF + 2 : HALF + 3] = b[4 * CUT : 4 * CUT + 1]
        out[d][HALF + 3 :] = jnp.zeros((5, E), f32)


def fold(*operands):
    anywhere = pl.BlockSpec(memory_space=pl.ANY)
    return pl.pallas_call(
        fold_kernel,
        in_specs=[VMEM] * 5 + [anywhere],
        out_specs=[anywhere] + [VMEM] * 4,
        out_shape=[shape(ZN, ROWS, E)] + [shape(HALF + 8, E)] * 4,
        input_output_aliases={5: 0},
        compiler_params=params(10),
        name="fold",
    )(*operands)


def land_kernel(m0, m1, m2, m3, out):
    out[...] = (m0[...] + m2[...]) + (m1[...] + m3[...])


def join_kernel(pos_ref, mine, mine2, other, other2, out, loss):
    c = pos_ref[1]
    out[pl.ds(pl.multiple_of(c * HALF, HALF), HALF), :] = mine[:HALF] + mine2[:HALF]
    out[pl.ds(pl.multiple_of((1 - c) * HALF, HALF), HALF), :] = other[:HALF] + other2[:HALF]
    total = (mine[HALF : HALF + 1] + mine2[HALF : HALF + 1]) + (
        mine[HALF + 1 : HALF + 2] + mine[HALF + 2 : HALF + 3]
    )
    loss[0] = jnp.max(total) / 32768


def sum_kernel(got, out):
    total = got[0]
    for k in range(1, ZN):
        total += got[k]
    out[...] = total


def body(queries, items, labels):
    core, y_lo, x_at, z_at = (lax.axis_index(a) for a in ("c", "yl", "x", "z"))
    pos = jnp.stack([z_at, core, y_lo, x_at]).astype(jnp.int32)
    (q,) = small(start_kernel, [queries, labels.reshape(1, ROWS)], [shape(PAD, E)])
    (own,) = small(own_kernel, [pos, items], [shape(HALF, E)])
    mine, other, xh, xl = gather(pos, q, own, items)
    sm0, sm1, stat_m = forward(pos, xh, xl, mine)
    so0, so1, stat_o = forward(pos, xh, xl, other)
    (stats,) = small(spread_kernel, [stat_m, send(stat_o, dc=1)], [shape(ZN, 3, ZN, ROWS)])
    stats = lax.all_to_all(stats, "z", 0, 0, tiled=True)
    (lse,) = small(merge_kernel, [stats], [shape(2 * ZN, ROWS)])
    lse = [lse, send(lse, dc=1)]
    oo, up, down, first = backward_a(pos, xh, xl, mine, other, *lse, sm1, so0, so1)
    a, b = send(up, dy=1), send(down, dy=-1)
    o, g = backward_b(pos, first, xh, xl, mine, other, *lse, sm0, sm1, so0, send(oo, dc=1))
    o, m0, m1, m2, m3 = fold(*lse, g, a, b, o)
    o = lax.all_to_all(o, "z", 0, 0, tiled=True)
    m2, m1, m3 = send(m2, dx=2), send(m1, dx=1), send(m3, dx=-1)
    (own,) = small(land_kernel, [m0, m1, m2, m3], [shape(HALF + 8, E)])
    got = send(own, dy=2)
    near = send(own, dc=1)
    item_grad, loss = small(
        join_kernel, [pos, own, got, near, send(got, dc=1)], [shape(2 * HALF, E), shape(1)]
    )
    (query_grad,) = small(sum_kernel, [o], [shape(ROWS, E)])
    return loss.reshape(()), query_grad, item_grad


def solution(mesh):
    grid = Mesh(mesh.devices.reshape(2, 2, 2, 4, 8), AXES)
    corpus = ("yl", "x", "z")
    in_specs = (P(AXES, None), P(corpus, None), P(AXES))
    out_specs = (P(), P(AXES, None), P(corpus, None))
    return jax.shard_map(body, mesh=grid, in_specs=in_specs, out_specs=out_specs, check_vma=False)
```

```python
import jax
import jax.numpy as jnp
from jax import lax
from jax.experimental import pallas as pl
from jax.experimental.pallas import tpu as pltpu
from jax.sharding import Mesh, PartitionSpec as P

E = 256
ZN, XN, YN = 8, 4, 4
ROWS = 128
PAD = 136
HALF = 256
CUT = HALF // 2
N = 4
W = N * ROWS
STEPS = 8 // N
PIECES = 8
LOCAL = PIECES * HALF
AXES = ("yh", "c", "yl", "x", "z")
f32, bf16 = jnp.float32, jnp.bfloat16


def place(i):
    return (i >> 7) & 1, (i >> 6) & 1, (i >> 5) & 1, (i >> 3) & 3, i & 7


def index(yh, c, yl, x, z):
    return yh * 128 + c * 64 + yl * 32 + x * 8 + z


def pairs(dx=0, dy=0, dz=0, dc=0):
    out = []
    for i in range(256):
        yh, c, yl, x, z = place(i)
        y = (yh * 2 + yl + dy) % YN
        out.append((i, index(y >> 1, (c + dc) % 2, y & 1, (x + dx) % XN, (z + dz) % ZN)))
    return out


def send(a, **shift):
    return lax.ppermute(a, AXES, pairs(**shift))


def twin(a, axis, hops=1):
    up, down = pairs(**{axis: hops}), pairs(**{axis: -hops})
    return lax.ppermute(a, AXES, [(down if (i >> 6) & 1 else up)[i] for i in range(256)])


def split(a):
    hi = a.astype(bf16)
    return hi, (a - hi.astype(f32)).astype(bf16)


def dot(a, b, dims):
    return lax.dot_general(a, b, (dims, ((), ())), preferred_element_type=f32)


def cat(parts, axis):
    return jnp.concatenate(parts, axis=axis)


NT = ((1,), (1,))
NN = ((1,), (0,))
TN = ((0,), (0,))
SMEM = pl.BlockSpec(memory_space=pltpu.SMEM)
VMEM = pl.BlockSpec(memory_space=pltpu.VMEM)


def shape(*dims, dtype=f32):
    return jax.ShapeDtypeStruct(dims, dtype)


def params(mib):
    return pltpu.CompilerParams(vmem_limit_bytes=mib * 2**20)


def local_labels(pos_ref, q_ref):
    lab = cat([q_ref[k, ROWS : ROWS + 1, :ROWS] for k in range(N)], 1)
    lab = lab.astype(jnp.int32)
    z, c, yl, x = pos_ref[0], pos_ref[1], pos_ref[2], pos_ref[3]
    here = ((lab >> 9) & 7 == z) & ((lab >> 8) & 1 == c)
    piece = (((lab >> 14) ^ yl) & 1) * 4 + (((lab >> 12) & 3) - x & 3)
    return jnp.where(here, piece * HALF + (lab & 255), -1)


def query_rows(q_ref):
    return cat([q_ref[k, :ROWS, :] for k in range(N)], 0) * (E**-0.5)


def small(kernel, ins, outs, smem_out=()):
    return pl.pallas_call(
        kernel,
        in_specs=[SMEM if a.ndim == 1 else VMEM for a in ins],
        out_specs=[SMEM if len(o.shape) == 1 else VMEM for o in outs],
        out_shape=outs,
        compiler_params=params(10),
        name=kernel.__name__,
    )(*ins)


def at(start, n):
    return pl.ds(pl.multiple_of(start, 8), n)


def start_kernel(queries, labels, q):
    q[:ROWS, :] = queries[...]
    q[ROWS:, :ROWS] = jnp.broadcast_to(labels[...].astype(f32), (PAD - ROWS, ROWS))
    q[ROWS:, ROWS:] = jnp.zeros((PAD - ROWS, E - ROWS), f32)


def own_kernel(pos_ref, items, own):
    own[...] = items[at(pos_ref[1] * HALF, HALF), :]


def pair_kernel(pos_ref, mine, other, out):
    n, c = mine.shape[0], pos_ref[1]
    out[at(c * n, n), :] = mine[...]
    out[at((1 - c) * n, n), :] = other[...]


def part_kernel(pos_ref, both, *refs):
    *_, mine, other = refs
    n, c = mine.shape[0], pos_ref[1]
    mine[...] = both[at(c * n, n), :]
    other[...] = both[at((1 - c) * n, n), :]


def third_kernel(pos_ref, both, after, after2, mine):
    mine[...] = both[at(pos_ref[1] * PAD, PAD), :]


def cut_third(*operands):
    anywhere = pl.BlockSpec(memory_space=pl.ANY)
    return pl.pallas_call(
        third_kernel,
        in_specs=[SMEM, VMEM, anywhere, anywhere],
        out_specs=VMEM,
        out_shape=shape(PAD, E),
        compiler_params=params(10),
        name="third",
    )(*operands)


def stack_kernel(*refs):
    *parts, out = refs
    row = 0
    for ref in parts:
        n = ref.shape[0]
        out[row : row + n, :] = ref[...]
        row += n


def pack_queries_kernel(pos_ref, q, qo, r2, r314, s2, s314, mine, other):
    z, c = pos_ref[0], pos_ref[1]
    mine[z], other[z] = q[...], qo[...]
    mine[(z + 4) & 7], other[(z + 4) & 7] = r314[4 * PAD :, :], s314[4 * PAD :, :]
    for k, r, s, row in ((2, r2, s2, 0), (3, r314, s314, 0), (1, r314, s314, 2 * PAD)):
        step = k - 2 * c * k
        for ref, where in ((r, (z - step) & 7), (s, (z + step) & 7)):
            mine[where] = ref[at(row + c * PAD, PAD), :]
            other[where] = ref[at(row + (1 - c) * PAD, PAD), :]


def pack_items_kernel(pos_ref, after, own, near, across, far, y_own, y_rest, xh, xl):
    c = pos_ref[1]

    def put(slot, rows):
        xh[at(slot * HALF, HALF), :], xl[at(slot * HALF, HALF), :] = split(rows)

    put(0, own[...])
    put(3 - 2 * c, near[...])
    put(1 + 2 * c, across[...])
    put(2, far[...])
    put(4, y_own[...])
    put(7 - 2 * c, y_rest[:HALF, :])
    put(5 + 2 * c, y_rest[HALF : 2 * HALF, :])
    put(6, y_rest[2 * HALF :, :])


def pack_items(*operands):
    return pl.pallas_call(
        pack_items_kernel,
        in_specs=[SMEM, pl.BlockSpec(memory_space=pl.ANY)] + [VMEM] * 6,
        out_specs=[VMEM] * 2,
        out_shape=[shape(LOCAL, E, dtype=bf16)] * 2,
        compiler_params=params(10),
        name="pack_items",
    )(*operands)


def join_stats(a, b):
    best = jnp.maximum(a[0], b[0])
    return best, a[1] * jnp.exp(a[0] - best) + b[1] * jnp.exp(b[0] - best)


def spread_kernel(mine, got, out):
    best, total = join_stats(mine, got)
    for k in range(ZN):
        out[k, 0] = best
        out[k, 1] = total
        out[k, 2] = mine[2] + got[2]


def merge_kernel(got, out):
    best = got[0, 0]
    for k in range(1, ZN):
        best = jnp.maximum(best, got[k, 0])
    total = pick = jnp.zeros((ZN, ROWS), f32)
    for k in range(ZN):
        total += got[k, 1] * jnp.exp(got[k, 0] - best)
        pick += got[k, 2]
    lse = best + jnp.log(total)
    out[:ZN] = lse
    out[ZN:] = jnp.full((8, ROWS), jnp.sum(lse - pick), f32)


def line_loss(own, other):
    row = own[ZN : ZN + 1, :] + other[ZN : ZN + 1, :]
    return cat([row, row], 1)


def forward_kernel(pos_ref, xh, xl, q_ref, s0_ref, s1_ref, stat_ref):
    qh, ql = split(query_rows(q_ref))
    qcat = cat([qh, qh, ql], 1)
    lab = local_labels(pos_ref, q_ref)
    rows = lax.broadcasted_iota(jnp.int32, (HALF, W), 0)
    top = total = None
    pick = jnp.zeros((8, W), f32)
    for t in range(PIECES):
        at = slice(t * HALF, (t + 1) * HALF)
        s = dot(cat([xh[at], xl[at], xh[at]], 1), qcat, NT)
        (s0_ref, s1_ref)[t // 4][0, t % 4] = s
        pick += jnp.sum(jnp.where(rows == lab - t * HALF, s, 0.0).reshape(32, 8, W), axis=0)
        s = s.reshape(32, 8, W)
        best = jnp.max(s, axis=0)
        if top is None:
            total = jnp.sum(jnp.exp(s - best[None]), axis=0)
        else:
            best = jnp.maximum(top, best)
            total = total * jnp.exp(top - best) + jnp.sum(jnp.exp(s - best[None]), axis=0)
        top = best
    best = jnp.max(top, axis=0, keepdims=True)
    total = jnp.sum(total * jnp.exp(top - best), axis=0, keepdims=True)
    pick = jnp.sum(pick, axis=0, keepdims=True)
    for h in range(N):
        z = N * pl.program_id(0) + h
        at = slice(h * ROWS, (h + 1) * ROWS)
        stat_ref[0, pl.ds(z, 1), :] = best[:, at]
        stat_ref[1, pl.ds(z, 1), :] = total[:, at]
        stat_ref[2, pl.ds(z, 1), :] = pick[:, at]


def forward(pos, xh, xl, q):
    return pl.pallas_call(
        forward_kernel,
        grid=(STEPS,),
        in_specs=[
            SMEM,
            pl.BlockSpec((LOCAL, E), lambda i: (0, 0)),
            pl.BlockSpec((LOCAL, E), lambda i: (0, 0)),
            pl.BlockSpec((N, PAD, E), lambda i: (i, 0, 0)),
        ],
        out_specs=[
            pl.BlockSpec((1, 4, HALF, W), lambda i: (i, 0, 0, 0)),
            pl.BlockSpec((1, 4, HALF, W), lambda i: (i, 0, 0, 0)),
            pl.BlockSpec((3, ZN, ROWS), lambda i: (0, 0, 0)),
        ],
        out_shape=[shape(STEPS, 4, HALF, W)] * 2 + [shape(3, ZN, ROWS)],
        compiler_params=params(18),
        cost_estimate=pl.CostEstimate(flops=3 * 2**30, bytes_accessed=10 * 2**20, transcendentals=2**21),
        name="forward",
    )(pos, xh, xl, q)


def block(i, pos_ref, lse_ref, q_ref):
    qh, ql = split(query_rows(q_ref))
    lse = cat([lse_ref[pl.ds(N * i + k, 1), :] for k in range(N)], 1)
    return cat([qh, ql, qh], 0), local_labels(pos_ref, q_ref), lse


def delta(s, lse, rows, lab, at):
    p = jnp.exp(s - lse)
    return split(jnp.where(rows == lab - at, p - 1.0, p))


def gradients(g_acc, x, s, operands, first, count, tiles):
    qcat, lab, lse = operands
    rows = lax.broadcasted_iota(jnp.int32, (HALF, W), 0)
    o = jnp.zeros((W, E), f32)
    for t in tiles:
        at = slice(t * HALF, (t + 1) * HALF)
        dh, dl = delta(s[t // 4][0, t % 4], lse, rows, lab, t * HALF)
        if first <= t < first + count:
            g_acc[t - first] += dot(cat([dh, dh, dl], 1), qcat, NN)
        if x is not None:
            o += dot(cat([dh, dh, dl], 0), cat([x[0][at], x[1][at], x[0][at]], 0), TN)
    return o * (E**-0.5)


def backward_a_kernel(pos_ref, xh, xl, mine, other, lse_m, lse_o, sm1, so0, so1, oo, up, down, token, g_acc):
    i = pl.program_id(0)

    @pl.when(i == 0)
    def _():
        g_acc[...] = jnp.zeros_like(g_acc)
        token[0] = 0.0

    @pl.when(i < STEPS)
    def _():
        operands = block(i, pos_ref, lse_m, mine)
        gradients(g_acc, None, (None, sm1), operands, 4, 4, range(4, 8))

    @pl.when(i >= STEPS)
    def _():
        operands = block(i - STEPS, pos_ref, lse_o, other)
        o = gradients(g_acc, (xh, xl), (so0, so1), operands, 4, 4, range(8))
        for k in range(N):
            oo[k] = o[k * ROWS : (k + 1) * ROWS]

    @pl.when(i == 2 * STEPS - 1)
    def _():
        for d in range(4):
            up[d * CUT : (d + 1) * CUT, :] = g_acc[d, :CUT, :]
            down[d * CUT : (d + 1) * CUT, :] = g_acc[d, CUT:, :]
        up[4 * CUT :, :] = down[4 * CUT :, :] = jnp.broadcast_to(line_loss(lse_m, lse_o), (8, E))


def backward_b_kernel(pos_ref, token, xh, xl, mine, other, lse_m, lse_o, sm0, sm1, so0, got, om, g_ref):
    i = pl.program_id(0)

    @pl.when(i == 0)
    def _():
        g_ref[...] = jnp.zeros_like(g_ref)

    @pl.when(i < STEPS)
    def _():
        operands = block(i, pos_ref, lse_o, other)
        gradients(g_ref, None, (so0, None), operands, 0, 4, range(4))

    @pl.when(i >= STEPS)
    def _():
        operands = block(i - STEPS, pos_ref, lse_m, mine)
        o = gradients(g_ref, (xh, xl), (sm0, sm1), operands, 0, 4, range(8))
        for k in range(N):
            om[k] = o[k * ROWS : (k + 1) * ROWS] + got[k]


def whole(*dims):
    return pl.BlockSpec(dims, lambda i: (0,) * len(dims))


def early(*dims):
    return pl.BlockSpec(dims, lambda i: (jnp.minimum(i, STEPS - 1),) + (0,) * (len(dims) - 1))


def late(*dims):
    return pl.BlockSpec(dims, lambda i: (jnp.maximum(i, STEPS) - STEPS,) + (0,) * (len(dims) - 1))


X_SPEC = whole(LOCAL, E)
LSE = whole(2 * ZN, ROWS)
Q = (N, PAD, E)
S = (1, 4, HALF, W)


def backward_a(pos, *operands):
    return pl.pallas_call(
        backward_a_kernel,
        grid=(2 * STEPS,),
        in_specs=[SMEM, X_SPEC, X_SPEC, early(*Q), late(*Q), LSE, LSE]
        + [early(*S), late(*S), late(*S)],
        out_specs=[late(N, ROWS, E)] + [whole(4 * CUT + 8, E)] * 2 + [SMEM],
        out_shape=[shape(ZN, ROWS, E)] + [shape(4 * CUT + 8, E)] * 2 + [shape(1)],
        scratch_shapes=[pltpu.VMEM((4, HALF, E), f32)],
        compiler_params=params(24),
        cost_estimate=pl.CostEstimate(flops=6 * 2**30, bytes_accessed=16 * 2**20, transcendentals=3 * 2**20),
        name="backward_a",
    )(pos, *operands)


def backward_b(pos, *operands):
    return pl.pallas_call(
        backward_b_kernel,
        grid=(2 * STEPS,),
        in_specs=[SMEM, SMEM, X_SPEC, X_SPEC, late(*Q), early(*Q), LSE, LSE]
        + [late(*S), late(*S), early(*S), late(N, ROWS, E)],
        out_specs=[late(N, ROWS, E), whole(4, HALF, E)],
        out_shape=[shape(ZN, ROWS, E), shape(4, HALF, E)],
        compiler_params=params(24),
        cost_estimate=pl.CostEstimate(flops=6 * 2**30, bytes_accessed=16 * 2**20, transcendentals=3 * 2**20),
        name="backward_b",
    )(pos, *operands)


def gather(pos, q, own, items):
    two = shape(2 * PAD, E)
    half = shape(HALF, E)
    x1 = twin(items, "dx")
    qo = send(q, dc=1)
    (r0,) = small(pair_kernel, [pos, q, qo], [two])
    r2 = twin(r0, "dz", 2)
    far = twin(own, "dx", 2)
    y0 = twin(own, "dy")
    third = cut_third(pos, r2, y0, far)
    (r20,) = small(stack_kernel, [r2, r0], [shape(4 * PAD, E)])
    r31, q4 = twin(r20, "dz"), twin(third, "dz", 2)
    near, rest = small(part_kernel, [pos, x1, third], [half, half])
    across = send(rest, dc=1)
    (rest,) = small(stack_kernel, [near, across, far], [shape(3 * HALF, E)])
    y_rest = twin(rest, "dy")
    (r314,) = small(stack_kernel, [r31, q4], [shape(5 * PAD, E)])
    mine, other = small(
        pack_queries_kernel,
        [pos, q, qo, r2, r314, send(r2, dc=1), send(r314, dc=1)],
        [shape(ZN, PAD, E)] * 2,
    )
    xh, xl = pack_items(pos, mine, own, near, across, far, y0, y_rest)
    return mine, other, xh, xl


def fold_kernel(lse_m, lse_o, g, a, b, o, held, *out):
    for d in range(4):
        at = slice(d * CUT, (d + 1) * CUT)
        out[d][:CUT] = g[d, :CUT] + a[at]
        out[d][CUT:HALF] = g[d, CUT:] + b[at]
        out[d][HALF : HALF + 1] = line_loss(lse_m, lse_o)
        out[d][HALF + 1 : HALF + 2] = a[4 * CUT : 4 * CUT + 1]
        out[d][HALF + 2 : HALF + 3] = b[4 * CUT : 4 * CUT + 1]
        out[d][HALF + 3 :] = jnp.zeros((5, E), f32)


def fold(*operands):
    anywhere = pl.BlockSpec(memory_space=pl.ANY)
    return pl.pallas_call(
        fold_kernel,
        in_specs=[VMEM] * 5 + [anywhere],
        out_specs=[anywhere] + [VMEM] * 4,
        out_shape=[shape(ZN, ROWS, E)] + [shape(HALF + 8, E)] * 4,
        input_output_aliases={5: 0},
        compiler_params=params(10),
        name="fold",
    )(*operands)


def land_kernel(m0, m1, m2, m3, out):
    out[...] = (m0[...] + m2[...]) + (m1[...] + m3[...])


def join_kernel(pos_ref, mine, mine2, other, other2, out, loss):
    c = pos_ref[1]
    out[pl.ds(pl.multiple_of(c * HALF, HALF), HALF), :] = mine[:HALF] + mine2[:HALF]
    out[pl.ds(pl.multiple_of((1 - c) * HALF, HALF), HALF), :] = other[:HALF] + other2[:HALF]
    total = (mine[HALF : HALF + 1] + mine2[HALF : HALF + 1]) + (
        mine[HALF + 1 : HALF + 2] + mine[HALF + 2 : HALF + 3]
    )
    loss[0] = jnp.max(total) / 32768


def sum_kernel(got, out):
    total = got[0]
    for k in range(1, ZN):
        total += got[k]
    out[...] = total


def body(queries, items, labels):
    core, y_lo, x_at, z_at = (lax.axis_index(a) for a in ("c", "yl", "x", "z"))
    pos = jnp.stack([z_at, core, y_lo, x_at]).astype(jnp.int32)
    (q,) = small(start_kernel, [queries, labels.reshape(1, ROWS)], [shape(PAD, E)])
    (own,) = small(own_kernel, [pos, items], [shape(HALF, E)])
    mine, other, xh, xl = gather(pos, q, own, items)
    sm0, sm1, stat_m = forward(pos, xh, xl, mine)
    so0, so1, stat_o = forward(pos, xh, xl, other)
    (stats,) = small(spread_kernel, [stat_m, send(stat_o, dc=1)], [shape(ZN, 3, ZN, ROWS)])
    stats = lax.all_to_all(stats, "z", 0, 0, tiled=True)
    (lse,) = small(merge_kernel, [stats], [shape(2 * ZN, ROWS)])
    lse = [lse, send(lse, dc=1)]
    oo, up, down, first = backward_a(pos, xh, xl, mine, other, *lse, sm1, so0, so1)
    a, b = send(up, dy=1), send(down, dy=-1)
    o, g = backward_b(pos, first, xh, xl, mine, other, *lse, sm0, sm1, so0, send(oo, dc=1))
    o, m0, m1, m2, m3 = fold(*lse, g, a, b, o)
    o = lax.all_to_all(o, "z", 0, 0, tiled=True)
    m2, m1, m3 = send(m2, dx=2), send(m1, dx=1), send(m3, dx=-1)
    (own,) = small(land_kernel, [m0, m1, m2, m3], [shape(HALF + 8, E)])
    got = send(own, dy=2)
    near = send(own, dc=1)
    item_grad, loss = small(
        join_kernel, [pos, own, got, near, send(got, dc=1)], [shape(2 * HALF, E), shape(1)]
    )
    (query_grad,) = small(sum_kernel, [o], [shape(ROWS, E)])
    return loss.reshape(()), query_grad, item_grad


def solution(mesh):
    grid = Mesh(mesh.devices.reshape(2, 2, 2, 4, 8), AXES)
    corpus = ("yl", "x", "z")
    in_specs = (P(AXES, None), P(corpus, None), P(AXES))
    out_specs = (P(), P(AXES, None), P(corpus, None))
    return jax.shard_map(body, mesh=grid, in_specs=in_specs, out_specs=out_specs, check_vma=False)
```
